128 devices in a mesh: dp: 32 (over x_lo, z, y), tensor: 4 (over x_hi, core).
Axes of the slice: x: 4 (x_hi: 2, x_lo: 2; x = x_hi * 2 + x_lo), y: 4, z: 4, core: 2. Of those that a mesh axis runs over, the one named last changes fastest.
Arguments:
- tokens: bfloat16 [16384, 1024], P(('dp', 'tensor')), may hold values from -6 to 6
- seq_lens: int32 [32, 4], P('dp'), may hold values from 1 to 509, as said below
- norm_attn: float32 [1024], replicated, may hold values from 0.25 to 1.75
- w_query: bfloat16 [1024, 1024], P('dp', 'tensor'), may hold values from -0.1875 to 0.1875
- w_key: bfloat16 [1024, 512], P('dp', 'tensor'), may hold values from -0.1875 to 0.1875
- w_value: bfloat16 [1024, 512], P('dp', 'tensor'), may hold values from -0.1875 to 0.1875
- w_out: bfloat16 [1024, 1024], P('tensor', 'dp'), may hold values from -3 to 3
- query_gain: float32 [64], replicated, may hold values from 0.25 to 1.75
- key_gain: float32 [64], replicated, may hold values from 0.25 to 1.75
- norm_ffn: float32 [1024], replicated, may hold values from 0.25 to 1.75
- w_gate: bfloat16 [1024, 4608], P('dp', 'tensor'), may hold values from -0.1875 to 0.1875
- w_up: bfloat16 [1024, 4608], P('dp', 'tensor'), may hold values from -0.1875 to 0.1875
- w_down: bfloat16 [4608, 1024], P('tensor', 'dp'), may hold values from -0.09375 to 0.09375
- cotangent: bfloat16 [16384, 1024], P(('dp', 'tensor')), may hold values from -6 to 6
Outputs:
- output: bfloat16 [16384, 1024], P(('dp', 'tensor'))
- grad_tokens: float32 [16384, 1024], P(('dp', 'tensor'))
- grad_norm_attn: float32 [1024], replicated
- grad_w_query: float32 [1024, 1024], P('dp', 'tensor')
- grad_w_key: float32 [1024, 512], P('dp', 'tensor')
- grad_w_value: float32 [1024, 512], P('dp', 'tensor')
- grad_w_out: float32 [1024, 1024], P('tensor', 'dp')
- grad_query_gain: float32 [64], replicated
- grad_key_gain: float32 [64], replicated
- grad_norm_ffn: float32 [1024], replicated
- grad_w_gate: float32 [1024, 4608], P('dp', 'tensor')
- grad_w_up: float32 [1024, 4608], P('dp', 'tensor')
- grad_w_down: float32 [4608, 1024], P('tensor', 'dp')
The draws below stay inside these ranges and needn't reach their ends.
Inputs may be any that keep to these rules, and one draw needn't show every extreme that they name: `seq_lens`: each row lists the lengths of the 4 sequences of one dp rank in packing order; they sum to 512, and one of them is longer than 384.
All inputs are finite; a program needn't handle non-finite values.
Results may differ from the reference program's by a relative error of at most 0.025.
Values may be sent and summed in bfloat16 or wider, within the bound.
A program may use at most 128 MiB of HBM per device.

```python
import math
import jax
import jax.numpy as jnp
from jax import lax

D = 1024
H = 16
KV = 8
HD = 64
FF = 4608
TOK_DP = 512
SEQS = 4
BLOCK = 512
RANKS = 32
TOKENS = 16384


def draw_seq_lens(key, part):
    key = jax.random.fold_in(key, 7)
    keys = jax.random.split(key, 5)
    longest = jax.random.randint(keys[0], (RANKS,), 3 * TOK_DP // 4 + 1, TOK_DP - SEQS + 2)
    chosen = jax.random.randint(keys[1], (), 0, RANKS)
    ranks = jnp.arange(RANKS, dtype=jnp.int32)
    longest = jnp.where(ranks == chosen, TOK_DP - SEQS + 1, longest)
    rest = TOK_DP - longest
    first = jax.random.randint(keys[2], (RANKS,), 1, rest - 1)
    second = jax.random.randint(keys[3], (RANKS,), 1, rest - first)
    third = rest - first - second
    place = jax.random.randint(keys[4], (RANKS,), 0, SEQS)
    others = jnp.stack([first, second, third], axis=1)
    slots = jnp.arange(SEQS, dtype=jnp.int32)[None, :]
    pick = jnp.clip(slots - (slots > place[:, None]).astype(jnp.int32), 0, SEQS - 2)
    filled = jnp.take_along_axis(others, pick, axis=1)
    return jnp.where(slots == place[:, None], longest[:, None], filled).astype(jnp.int32)


def shard_levels(stream_key, extent, cuts, smallest, high):
    factor_of = 1.0
    for dim, blocks in cuts:
        draws = jax.random.uniform(jax.random.fold_in(jax.random.fold_in(stream_key, 6), dim), (blocks,), jnp.float32, smallest / len(cuts), high / len(cuts))
        factor_of = factor_of * jnp.repeat(jnp.exp(draws), extent[dim] // blocks).reshape((-1,) + (1,) * (len(extent) - 1 - dim))
    return factor_of


def scatter_about(key, shape, scale, bound, cuts=(), held_as=jnp.bfloat16):
    values = jax.random.normal(key, shape, jnp.float32) * scale
    if len(cuts) > 0:
        values = shard_levels(key, shape, cuts, -0.22, 0.18) * values
    return jnp.clip(values, min=-bound, max=bound).astype(held_as)


def setup_inputs(seed: int = 0) -> dict:
    seeds = jax.random.split(jax.random.key(seed), 15)
    return {
        "tokens": scatter_about(seeds[0], (TOKENS, D), 1.0, 6.0, ((0, 128),)),
        "seq_lens": draw_seq_lens(jax.random.fold_in(seeds[14], 71), 0),
        "norm_attn": jnp.clip(1.0 + 0.15 * jax.random.normal(seeds[2], (D,), jnp.float32), 0.25, 1.75),
        "w_query": scatter_about(seeds[3], (D, H * HD), D ** -0.5, 0.1875, ((0, 32), (1, 4))),
        "w_key": scatter_about(seeds[4], (D, KV * HD), D ** -0.5, 0.1875, ((0, 32), (1, 4))),
        "w_value": scatter_about(seeds[5], (D, KV * HD), D ** -0.5, 0.1875, ((0, 32), (1, 4))),
        "w_out": scatter_about(seeds[6], (H * HD, D), (max(H * HD // 256, 1)) ** -0.5, 3.0, ((0, 4), (1, 32))),
        "query_gain": jnp.clip(1.0 + 0.15 * jax.random.normal(seeds[7], (HD,), jnp.float32), 0.25, 1.75),
        "key_gain": jnp.clip(1.0 + 0.15 * jax.random.normal(seeds[8], (HD,), jnp.float32), 0.25, 1.75),
        "norm_ffn": jnp.clip(1.0 + 0.15 * jax.random.normal(seeds[9], (D,), jnp.float32), 0.25, 1.75),
        "w_gate": scatter_about(seeds[10], (D, FF), D ** -0.5, 0.1875, ((0, 32), (1, 4))),
        "w_up": scatter_about(seeds[11], (D, FF), D ** -0.5, 0.1875, ((0, 32), (1, 4))),
        "w_down": scatter_about(seeds[12], (FF, D), FF ** -0.5, 0.09375, ((0, 4), (1, 32))),
        "cotangent": scatter_about(seeds[13], (TOKENS, D), 1.0, 6.0, ((0, 128),)),
    }


@jax.custom_vjp
def low(v):
    return lax.optimization_barrier(v.astype(jnp.bfloat16)).astype(jnp.float32)

@jax.custom_vjp
def low_back(v):
    return v

def low_keep(v):
    return (low(v), None)

def low_pass(kept, grad):
    return (grad,)

def back_keep(v):
    return (v, None)

def back_low(kept, grad):
    return (low(grad),)
low.defvjp(low_keep, low_pass)
low_back.defvjp(back_keep, back_low)
epsilon = 1e-05
theta = 1000000.0
highest = lax.Precision.HIGHEST

def rmsnorm(values):
    return values * lax.rsqrt(lax.optimization_barrier(jnp.mean(values * values, axis=-1, keepdims=True)) + epsilon)

def matmul(left, right):
    return jnp.dot(left, right, precision=highest)

def layout(seq_lens, rows):
    ends = jnp.cumsum(seq_lens).astype(jnp.int32)
    starts = (ends - seq_lens).astype(jnp.int32)
    index = jnp.arange(rows, dtype=jnp.int32)
    segment = lax.optimization_barrier(jnp.sum((index[:, None] >= ends[None, :]).astype(jnp.int32), axis=1))
    owner = segment[:, None] == jnp.arange(seq_lens.shape[0], dtype=jnp.int32)[None, :]
    offset = lax.optimization_barrier(jnp.sum(jnp.where(owner, starts[None, :], 0), axis=1)).astype(jnp.int32)
    return (segment, (index - offset).astype(jnp.int32))

def tables(position, width):
    half = width // 2
    freq = jnp.exp(-math.log(theta) * 2.0 * jnp.arange(half, dtype=jnp.float32) / width)
    angle = position.astype(jnp.float32)[:, None] * freq[None, :]
    return (jnp.cos(angle)[:, None, :], jnp.sin(angle)[:, None, :])

def rotate(values, cosine, sine):
    half = values.shape[-1] // 2
    first = values[..., :half]
    second = values[..., half:]
    return jnp.concatenate([first * cosine - second * sine, second * cosine + first * sine], axis=-1)

def visible(segment, start, count):
    rows = segment.shape[0]
    query_index = start + jnp.arange(count, dtype=jnp.int32)
    key_index = jnp.arange(rows, dtype=jnp.int32)
    query_seg = lax.dynamic_slice_in_dim(segment, start, count)
    return (query_seg[:, None] == segment[None, :]) & (key_index[None, :] <= query_index[:, None])

def attend(qblock, start, key_rot, value_rot, segment):
    scale = qblock.shape[-1] ** (-0.5)
    raw = low_back(jnp.einsum('bkgd,skd->kgbs', qblock, key_rot, precision=highest))
    allowed = visible(segment, start, qblock.shape[0])
    scores = jnp.where(allowed, raw * scale, -1e+30)
    top = lax.optimization_barrier(jnp.max(scores, axis=-1, keepdims=True))
    expo = jnp.exp(scores - top)
    probs = low(expo / lax.optimization_barrier(jnp.sum(expo, axis=-1, keepdims=True)))
    return low(low_back(jnp.einsum('kgbs,skd->bkgd', probs, value_rot, precision=highest)))

def forward(tokens, weights, segment, position):
    norm_attn, w_query, w_key, w_value, w_out, query_gain, key_gain, norm_ffn, w_gate, w_up, w_down = weights
    rows = tokens.shape[0]
    head = query_gain.shape[0]
    group = H // KV
    input_one = low(rmsnorm(tokens) * norm_attn)
    query_raw = low_back(matmul(input_one, w_query)).reshape(rows, H, head)
    key_raw = low_back(matmul(input_one, w_key)).reshape(rows, KV, head)
    value_rot = low(low_back(matmul(input_one, w_value))).reshape(rows, KV, head)
    cosine, sine = tables(position, head)
    query_rot = low(rotate(rmsnorm(query_raw) * query_gain, cosine, sine)).reshape(rows, KV, group, head)
    key_rot = low(rotate(rmsnorm(key_raw) * key_gain, cosine, sine))
    count = rows // BLOCK
    blocks = query_rot.reshape(count, BLOCK, KV, group, head)
    starts = jnp.arange(count, dtype=jnp.int32) * BLOCK

    def one_block(item):
        return attend(item[0], item[1], key_rot, value_rot, segment)
    attended = lax.map(jax.checkpoint(one_block), (blocks, starts)).reshape(rows, H * head)
    middle = tokens + low_back(matmul(attended, w_out))
    input_two = low(rmsnorm(middle) * norm_ffn)
    gate = low_back(matmul(input_two, w_gate))
    up = low_back(matmul(input_two, w_up))
    hidden = low(jax.nn.silu(gate) * up)
    return middle + low_back(matmul(hidden, w_down))

def reference(tokens, seq_lens, norm_attn, w_query, w_key, w_value, w_out, query_gain, key_gain, norm_ffn, w_gate, w_up, w_down, cotangent):
    weights = (norm_attn.astype(jnp.float32), w_query.astype(jnp.float32), w_key.astype(jnp.float32), w_value.astype(jnp.float32), w_out.astype(jnp.float32), query_gain.astype(jnp.float32), key_gain.astype(jnp.float32), norm_ffn.astype(jnp.float32), w_gate.astype(jnp.float32), w_up.astype(jnp.float32), w_down.astype(jnp.float32))
    inputs = tokens.astype(jnp.float32).reshape(RANKS, TOK_DP, D)
    grads_in = cotangent.astype(jnp.float32).reshape(RANKS, TOK_DP, D)

    def step(totals, item):
        rank_tokens, rank_grad, rank_lens = item
        segment, position = layout(rank_lens, TOK_DP)

        def run(values, *params):
            return forward(values, params, segment, position)
        result, pull = jax.vjp(run, rank_tokens, *weights)
        grads = pull(rank_grad)
        totals = tuple((a + b for a, b in zip(totals, grads[1:])))
        return (totals, (result.astype(jnp.bfloat16), grads[0]))
    zero = tuple((jnp.zeros_like(w) for w in weights))
    totals, (outputs, grad_rows) = lax.scan(step, zero, (inputs, grads_in, seq_lens))
    return (outputs.reshape(TOKENS, D), grad_rows.reshape(TOKENS, D), totals[0], totals[1], totals[2], totals[3], totals[4], totals[5], totals[6], totals[7], totals[8], totals[9], totals[10])
```

```python
import functools
import math

import jax
import jax.numpy as jnp
import numpy as np
from jax import lax
from jax.experimental import pallas as pl
from jax.experimental.pallas import tpu as pltpu
from jax.sharding import PartitionSpec as P

MESH = pl.DeviceIdType.MESH
BF = jnp.bfloat16
F32 = jnp.float32

D = 1024
HD = 64
FF_PARTS = (384, 384, 384)
FF_OFF = tuple(int(v) for v in np.cumsum((0,) + FF_PARTS)[:-1])
WIDTHS = (768,) + tuple(3 * c for c in FF_PARTS)
CHUNKS = len(WIDTHS)
FFL = sum(FF_PARTS)
EPS = 1e-05
THETA = 1000000.0
GAINS = 2304
NSEM = 34 * CHUNKS + 40

LO = pl.ds(0, 16)
HI = pl.ds(16, 16)


def dot(a, b):
    return jnp.dot(a, b, preferred_element_type=F32)


def dot_nt(a, b):
    return lax.dot_general(a, b, (((1,), (1,)), ((), ())), preferred_element_type=F32)


def dot_tn(a, b):
    return lax.dot_general(a, b, (((0,), (0,)), ((), ())), preferred_element_type=F32)


def rms(v):
    inverse = lax.rsqrt(jnp.mean(v * v, axis=-1, keepdims=True) + EPS)
    return v * inverse, inverse


def kernel(
    lens, tok, cot, wq, wk, wv, wo, wg, wu, wd, na, nf, qg, kg, fr,
    out, gtok, gq_w, gk_w, gv_w, go_w, gg_w, gu_w, gd_w, gains,
    Ws, Gs, RA, RB, RC, RD, RE,
    A1, A2, GO, GX, A1T, A2T, GOT,
    PB, T1, T2, X2, DX2,
    COS, SIN, BIAS, NQ, RQ, QS, KD, VD, PR, O, DO, DQ, DK, DV, DQKV,
    HID, DG, DU, DA, GV,
    ssem, rsem,
):
    me = lax.axis_index("dp")
    t = lax.axis_index("tensor")
    x = me // 16
    z = (me // 4) % 4
    y = me % 4
    xo = (x + 1) % 2
    zl, zr, zo = (z + 3) % 4, (z + 1) % 4, (z + 2) % 4
    yl, yr, yo = (y + 3) % 4, (y + 1) % 4, (y + 2) % 4
    ts = t + 1 - 2 * (t % 2)
    to = (t + 2) % 4
    td = (ts + 2) % 4

    def dp(xx, zz, yy):
        return (xx * 16 + zz * 4 + yy, t)

    d_x = dp(xo, z, y)
    d_zl, d_zr, d_zo = dp(x, zl, y), dp(x, zr, y), dp(x, zo, y)
    d_yl, d_yr, d_yo = dp(x, z, yl), dp(x, z, yr), dp(x, z, yo)
    d_s, d_o, d_d = (me, ts), (me, to), (me, td)
    partners = (d_x, d_zl, d_zr, d_zo, d_yl, d_yr, d_yo, d_s, d_o, d_d)

    started = []

    def send(src, dst, device):
        index = len(started)
        copy = pltpu.make_async_remote_copy(
            src_ref=src,
            dst_ref=dst,
            send_sem=ssem.at[index],
            recv_sem=rsem.at[index],
            device_id=device,
            device_id_type=MESH,
        )
        copy.start()
        started.append(copy)
        return copy

    ag = {}

    def ag0(c):
        W = Ws[c]
        ag[c, 0] = send(W.at[x, z, y], W.at[x, z, y], d_x)

    def ag1(c):
        W = Ws[c]
        ag[c, 0].wait_recv()
        a, b = W.at[:, z, y, LO], W.at[:, z, y, HI]
        ag[c, 1] = (send(a, a, d_zr), send(a, a, d_zl), send(b, b, d_yr), send(b, b, d_yl))

    def ag2(c):
        W, r = Ws[c], ag[c, 1]
        r[0].wait_recv()
        v = W.at[0, zl, y, LO]
        f0 = send(v, v, d_zr)
        r[2].wait_recv()
        v = W.at[0, z, yl, HI]
        f2 = send(v, v, d_yr)
        r[1].wait_recv()
        v = W.at[1, zr, y, LO]
        f1 = send(v, v, d_zl)
        r[3].wait_recv()
        v = W.at[1, z, yr, HI]
        f3 = send(v, v, d_yl)
        ag[c, 2] = (f0, f1, f2, f3)

    def ag3(c):
        W, r = Ws[c], ag[c, 2]
        r[0].wait_recv()
        r[1].wait_recv()
        a = W.at[:, :, y, LO]
        f0, f1 = send(a, a, d_yr), send(a, a, d_yl)
        r[2].wait_recv()
        r[3].wait_recv()
        b = W.at[:, z, :, HI]
        ag[c, 3] = (f0, f1, send(b, b, d_zr), send(b, b, d_zl))

    def ag4(c):
        W, r = Ws[c], ag[c, 3]
        r[0].wait_recv()
        v = W.at[0, :, yl, LO]
        f0 = send(v, v, d_yr)
        r[2].wait_recv()
        v = W.at[0, zl, :, HI]
        f2 = send(v, v, d_zr)
        r[1].wait_recv()
        v = W.at[1, :, yr, LO]
        f1 = send(v, v, d_yl)
        r[3].wait_recv()
        v = W.at[1, zr, :, HI]
        f3 = send(v, v, d_zl)
        ag[c, 4] = (f0, f1, f2, f3)

    def ag5(c):
        for copy in ag[c, 4]:
            copy.wait_recv()

    ag_steps = (ag0, ag1, ag2, ag3, ag4, ag5)

    rs = {}

    def add(ref, index, *others):
        total = ref[index].astype(F32)
        for other in others:
            total = total + other.astype(F32).reshape(total.shape)
        ref[index] = total.astype(BF)

    lo, hi = slice(0, 16), slice(16, 32)
    every = slice(None)

    def one(i):
        return pl.ds(i, 1)

    def rs1(c):
        G, ra = Gs[c], RA[c]
        rs[c, 1] = (
            send(G.at[0, :, yo, LO], ra.at[0, 0], d_yr),
            send(G.at[1, :, yo, LO], ra.at[0, 1], d_yl),
            send(G.at[0, zo, :, HI], ra.at[1, 0], d_zr),
            send(G.at[1, zo, :, HI], ra.at[1, 1], d_zl),
        )

    def rs2(c):
        G, ra, rb, r = Gs[c], RA[c], RB[c], rs[c, 1]
        r[0].wait_recv()
        add(G, (0, every, one(yr), lo), ra[0, 0])
        f0 = send(G.at[:, :, yr, LO], rb.at[0, 0], d_yr)
        r[2].wait_recv()
        add(G, (0, one(zr), every, hi), ra[1, 0])
        f2 = send(G.at[:, zr, :, HI], rb.at[1, 0], d_zr)
        r[1].wait_recv()
        add(G, (1, every, one(yl), lo), ra[0, 1])
        f1 = send(G.at[:, :, yl, LO], rb.at[0, 1], d_yl)
        r[3].wait_recv()
        add(G, (1, one(zl), every, hi), ra[1, 1])
        f3 = send(G.at[:, zl, :, HI], rb.at[1, 1], d_zl)
        rs[c, 2] = (f0, f1, f2, f3)

    def rs3(c):
        G, rb, rc, r = Gs[c], RB[c], RC[c], rs[c, 2]
        r[0].wait_recv()
        r[1].wait_recv()
        add(G, (every, every, one(y), lo), rb[0, 0], rb[0, 1])
        f0 = send(G.at[0, zo, y, LO], rc.at[0, 0], d_zr)
        f1 = send(G.at[1, zo, y, LO], rc.at[0, 1], d_zl)
        r[2].wait_recv()
        r[3].wait_recv()
        add(G, (every, one(z), every, hi), rb[1, 0], rb[1, 1])
        f2 = send(G.at[0, z, yo, HI], rc.at[1, 0], d_yr)
        f3 = send(G.at[1, z, yo, HI], rc.at[1, 1], d_yl)
        rs[c, 3] = (f0, f1, f2, f3)

    def rs4(c):
        G, rc, rd, r = Gs[c], RC[c], RD[c], rs[c, 3]
        r[0].wait_recv()
        add(G, (0, one(zr), one(y), lo), rc[0, 0])
        f0 = send(G.at[:, zr, y, LO], rd.at[0, 0], d_zr)
        r[2].wait_recv()
        add(G, (0, one(z), one(yr), hi), rc[1, 0])
        f2 = send(G.at[:, z, yr, HI], rd.at[1, 0], d_yr)
        r[1].wait_recv()
        add(G, (1, one(zl), one(y), lo), rc[0, 1])
        f1 = send(G.at[:, zl, y, LO], rd.at[0, 1], d_zl)
        r[3].wait_recv()
        add(G, (1, one(z), one(yl), hi), rc[1, 1])
        f3 = send(G.at[:, z, yl, HI], rd.at[1, 1], d_yl)
        rs[c, 4] = (f0, f1, f2, f3)

    def rs5(c):
        G, rd, r = Gs[c], RD[c], rs[c, 4]
        for copy in r:
            copy.wait_recv()
        add(G, (every, one(z), one(y), lo), rd[0, 0], rd[0, 1])
        add(G, (every, one(z), one(y), hi), rd[1, 0], rd[1, 1])
        rs[c, 5] = send(G.at[xo, z, y], RE[c], d_x)

    def rs6(c):
        rs[c, 5].wait_recv()
        total = Gs[c][x, z, y].astype(F32) + RE[c][...].astype(F32)
        if c == 0:
            gq_w[...] = total[:, 0:256]
            gk_w[...] = total[:, 256:384]
            gv_w[...] = total[:, 384:512]
            go_w[...] = total[:, 512:768]
        else:
            w, o = FF_PARTS[c - 1], FF_OFF[c - 1]
            gg_w[:, o : o + w] = total[:, 0:w]
            gu_w[:, o : o + w] = total[:, w : 2 * w]
            gd_w[:, o : o + w] = total[:, 2 * w : 3 * w]

    rs_steps = (None, rs1, rs2, rs3, rs4, rs5, rs6)

    def rows_start(buf):
        v = buf.at[t]
        return send(v, v, d_o), send(v, v, d_s)

    def rows_relay(buf, pair):
        pair[0].wait_recv()
        v = buf.at[to]
        return send(v, v, d_s)

    def rows_end(pair, relay):
        pair[1].wait_recv()
        relay.wait_recv()

    def sum_start(k, part):
        PB[k, td] = part(td)
        c0 = send(PB.at[k, td], T1.at[k, 1], d_s)
        PB[k, ts] = part(ts)
        c1 = send(PB.at[k, ts], T1.at[k, 0], d_s)
        PB[k, to] = part(to)
        PB[k, t] = part(t)
        return c0, c1

    def sum_mid(k, copies):
        copies[0].wait_recv()
        PB[k, to] = (PB[k, to].astype(F32) + T1[k, 1].astype(F32)).astype(BF)
        return send(PB.at[k, to], T2.at[k], d_o)

    def sum_end(k, copies, last):
        copies[1].wait_recv()
        part = PB[k, t].astype(F32) + T1[k, 0].astype(F32)
        last.wait_recv()
        return part + T2[k].astype(F32)

    barrier = pltpu.get_barrier_semaphore()
    for device in partners:
        pl.semaphore_signal(barrier, inc=1, device_id=device, device_id_type=MESH)

    W0 = Ws[0]
    W0[x, z, y, :, 0:256] = wq[...]
    W0[x, z, y, :, 256:384] = wk[...]
    W0[x, z, y, :, 384:512] = wv[...]
    W0[x, z, y, :, 512:768] = wo[...]
    for c in range(1, CHUNKS):
        w, o = FF_PARTS[c - 1], FF_OFF[c - 1]
        Ws[c][x, z, y, :, 0:w] = wg[:, o : o + w]
        Ws[c][x, z, y, :, w : 2 * w] = wu[:, o : o + w]
        Ws[c][x, z, y, :, 2 * w : 3 * w] = wd[:, o : o + w]
    n1, _ = rms(tok[...].astype(F32))
    A1[t] = (n1 * na[...]).astype(BF)
    GO[t] = cot[...]

    pl.semaphore_wait(barrier, len(partners))

    ag0(0)
    a1_pair = rows_start(A1)
    for c in range(1, CHUNKS):
        ag0(c)

    lane = lax.broadcasted_iota(jnp.int32, (1, 128), 1)
    left_head = lane < 64
    first_half = (lane % 64) < 32

    e1 = lens[0, 0]
    e2 = e1 + lens[0, 1]
    e3 = e2 + lens[0, 2]

    def begin(row):
        return jnp.where(
            row >= e3, e3, jnp.where(row >= e2, e2, jnp.where(row >= e1, e1, 0))
        )

    def fill_tables(i, carry):
        rows = pl.ds(pl.multiple_of(i * 128, 128), 128)
        row = lax.broadcasted_iota(jnp.int32, (128, 128), 0) + i * 128
        angle = (row - begin(row)).astype(F32) * fr[...]
        COS[rows] = jnp.cos(angle)
        SIN[rows] = jnp.where(first_half, -1.0, 1.0) * jnp.sin(angle)
        return carry

    def fill_bias(i, carry):
        rows = pl.ds(pl.multiple_of(i * 128, 128), 128)
        row = lax.broadcasted_iota(jnp.int32, (128, 512), 0) + i * 128
        col = lax.broadcasted_iota(jnp.int32, (128, 512), 1)
        seen = (col <= row) & (col >= begin(row))
        BIAS[rows] = jnp.where(seen, 0.0, -1e30)
        return carry

    ag1(0)
    lax.fori_loop(0, 4, fill_tables, 0)
    a1_relay = rows_relay(A1, a1_pair)
    ag2(0)
    go_pair = rows_start(GO)
    ag1(1)
    lax.fori_loop(0, 4, fill_bias, 0)
    ag3(0)
    rows_end(a1_pair, a1_relay)
    ag2(1)
    A1T[...] = A1[...].reshape(512, D).T
    go_relay = rows_relay(GO, go_pair)
    for c in range(2, CHUNKS):
        ag1(c)
    ag4(0)
    ag3(1)
    rows_end(go_pair, go_relay)
    GOT[...] = GO[...].reshape(512, D).T
    ag5(0)

    def rope(v, rows):
        swapped = jnp.where(first_half, pltpu.roll(v, 96, 1), pltpu.roll(v, 32, 1))
        return v * COS[rows] + swapped * SIN[rows]

    def rope_back(v, rows):
        swapped = jnp.where(first_half, pltpu.roll(v, 96, 1), pltpu.roll(v, 32, 1))
        return v * COS[rows] - swapped * SIN[rows]

    hr = lax.broadcasted_iota(jnp.int32, (128, 128), 0) // 64
    hc = lax.broadcasted_iota(jnp.int32, (128, 128), 1) // 64
    mean_of = jnp.where(hr == hc, 1.0 / HD, 0.0).astype(BF)

    def head_mean(v):
        high = v.astype(BF)
        low = (v - high.astype(F32)).astype(BF)
        return dot(high, mean_of) + dot(low, mean_of)

    q_gain = jnp.concatenate([qg[...], qg[...]], axis=1)
    k_gain = jnp.concatenate([kg[...], kg[...]], axis=1)

    def qkv_block(i, carry):
        rows = pl.ds(pl.multiple_of(i * 256, 256), 256)
        raw = dot(A1[pl.ds(2 * i, 2)].reshape(256, D), W0[:, :, :, :, 0:512].reshape(D, 512))
        for g in range(3):
            v = raw[:, 128 * g : 128 * g + 128]
            inverse = lax.rsqrt(head_mean(v * v) + EPS)
            n = v * inverse
            NQ[g, rows] = n
            RQ[g, rows] = inverse
            r = rope(n * (q_gain if g < 2 else k_gain), rows)
            if g < 2:
                QS[g, rows] = (r * HD**-0.5).astype(BF)
            else:
                turned = pltpu.roll(r, 64, 1)
                KD[0, rows] = jnp.where(left_head, r, turned).astype(BF)
                KD[1, rows] = jnp.where(left_head, turned, r).astype(BF)
        v = raw[:, 384:512]
        turned = pltpu.roll(v, 64, 1)
        VD[0, rows] = jnp.where(left_head, v, turned).astype(BF)
        VD[1, rows] = jnp.where(left_head, turned, v).astype(BF)
        return carry

    lax.fori_loop(0, 2, qkv_block, 0)

    def stack(v):
        none = jnp.zeros_like(v)
        return jnp.concatenate(
            [jnp.where(left_head, v, none), jnp.where(left_head, none, v)], axis=0
        )

    def unstack(v):
        half = v.shape[0] // 2
        return jnp.where(left_head, v[:half], v[half:])

    def attend(g, b):
        rows, keys = pl.ds(256 * b, 256), 256 * (b + 1)
        scores = dot_nt(stack(QS[g, rows]), KD[g, 0:keys])
        bias = BIAS[rows, 0:keys]
        scores = scores + jnp.concatenate([bias, bias], axis=0)
        expo = jnp.exp(scores - jnp.max(scores, axis=-1, keepdims=True))
        probs = expo * (1.0 / jnp.sum(expo, axis=-1, keepdims=True))
        PR[g, 512 * b : 512 * b + 512, 0:keys] = probs
        O[rows, 128 * g : 128 * g + 128] = unstack(dot(probs.astype(BF), VD[g, 0:keys])).astype(BF)

    ag4(1)
    attend(0, 0)
    attend(0, 1)
    ag2(2)
    attend(1, 0)
    attend(1, 1)
    ag3(2)

    def out_part(b):
        rows = pl.ds(pl.multiple_of(b * 128, 128), 128)
        return dot_nt(O[rows], W0[:, :, :, :, 512:768].reshape(D, 256)).astype(BF)

    at_copies = sum_start(0, out_part)
    for c in range(3, CHUNKS):
        ag2(c)
    at_last = sum_mid(0, at_copies)
    ag4(2)
    for c in range(3, CHUNKS):
        ag3(c)
    x2 = tok[...].astype(F32) + sum_end(0, at_copies, at_last)
    X2[...] = x2
    n2, _ = rms(x2)
    A2[t] = (n2 * nf[...]).astype(BF)
    a2_pair = rows_start(A2)
    ag5(1)
    for c in range(3, CHUNKS):
        ag4(c)
    a2_relay = rows_relay(A2, a2_pair)
    rows_end(a2_pair, a2_relay)
    A2T[...] = A2[...].reshape(512, D).T

    def ffn_chunk(c):
        W, G = Ws[c], Gs[c]
        w, o = FF_PARTS[c - 1], FF_OFF[c - 1]
        cols = slice(o, o + w)

        def block(i, carry):
            rows = pl.ds(pl.multiple_of(i * 256, 256), 256)
            a = A2[pl.ds(2 * i, 2)].reshape(256, D)
            g = GO[pl.ds(2 * i, 2)].reshape(256, D)
            gate = dot(a, W[:, :, :, :, 0:w].reshape(D, w))
            up = dot(a, W[:, :, :, :, w : 2 * w].reshape(D, w))
            dhid = dot(g, W[:, :, :, :, 2 * w : 3 * w].reshape(D, w))
            sigma = jax.nn.sigmoid(gate)
            swish = gate * sigma
            HID[rows, cols] = (swish * up).astype(BF)
            dgate = (dhid * up * sigma * (1.0 + gate * (1.0 - sigma))).astype(BF)
            dup = (dhid * swish).astype(BF)
            DG[rows, cols] = dgate
            DU[rows, cols] = dup
            part = dot_nt(dgate, W[:, :, :, :, 0:w].reshape(D, w)) + dot_nt(
                dup, W[:, :, :, :, w : 2 * w].reshape(D, w)
            )
            if c == 1:
                DA[rows] = part
            else:
                DA[rows] = DA[rows] + part
            return carry

        lax.fori_loop(0, 2, block, 0)

    def ffn_grads(c):
        G = Gs[c]
        w, o = FF_PARTS[c - 1], FF_OFF[c - 1]
        cols = slice(o, o + w)

        def block(i, carry):
            rows = pl.ds(pl.multiple_of(i * 256, 256), 256)
            zs = pl.ds(2 * (i % 2), 2)
            a, g = A2T[rows], GOT[rows]
            G[i // 2, zs, :, :, 0:w] = dot(a, DG[:, cols]).astype(BF).reshape(2, 4, 32, w)
            G[i // 2, zs, :, :, w : 2 * w] = dot(a, DU[:, cols]).astype(BF).reshape(2, 4, 32, w)
            G[i // 2, zs, :, :, 2 * w : 3 * w] = dot(g, HID[:, cols]).astype(BF).reshape(2, 4, 32, w)
            return carry

        lax.fori_loop(0, 4, block, 0)

    for c in range(1, CHUNKS):
        if c > 1:
            ag5(c)
        ffn_chunk(c)
        if c + 1 < CHUNKS:
            ffn_grads(c)
            rs1(c)
            if c > 1:
                rs2(c - 1)

    def da2_part(b):
        rows = pl.ds(pl.multiple_of(b * 128, 128), 128)
        return DA[rows].astype(BF)

    da2_copies = sum_start(1, da2_part)
    ffn_grads(CHUNKS - 1)
    rs1(CHUNKS - 1)
    da2_last = sum_mid(1, da2_copies)
    if CHUNKS > 2:
        rs2(CHUNKS - 2)

    def y_part(b):
        rows = pl.ds(pl.multiple_of(b * 128, 128), 128)
        total = None
        for c in range(1, CHUNKS):
            w, o = FF_PARTS[c - 1], FF_OFF[c - 1]
            part = dot_nt(HID[rows, o : o + w], Ws[c][:, :, :, :, 2 * w : 3 * w].reshape(D, w))
            total = part if total is None else total + part
        return total.astype(BF)

    y_copies = sum_start(2, y_part)

    da2 = sum_end(1, da2_copies, da2_last)
    n2, r2 = rms(X2[...])
    GV[0, pl.ds(t, 1), :, 1024:2048] = jnp.sum(da2 * n2, axis=0, keepdims=True).reshape(1, 1, D)
    h = da2 * nf[...]
    dx2 = cot[...].astype(F32) + r2 * (h - n2 * jnp.mean(h * n2, axis=-1, keepdims=True))
    DX2[...] = dx2
    GX[t] = dx2.astype(BF)
    gx_pair = rows_start(GX)
    rs2(CHUNKS - 1)
    gx_relay = rows_relay(GX, gx_pair)
    y_last = sum_mid(2, y_copies)
    if CHUNKS > 2:
        rs3(1)
    rows_end(gx_pair, gx_relay)

    def do_block(i, carry):
        rows = pl.ds(pl.multiple_of(i * 256, 256), 256)
        g = GX[pl.ds(2 * i, 2)].reshape(256, D)
        DO[rows] = dot(g, W0[:, :, :, :, 512:768].reshape(D, 256)).astype(BF)
        return carry

    lax.fori_loop(0, 2, do_block, 0)

    def attend_back(g, b):
        rows, keys = pl.ds(256 * b, 256), 256 * (b + 1)
        qs = stack(QS[g, rows])
        dos = stack(DO[rows, 128 * g : 128 * g + 128])
        probs = PR[g, 512 * b : 512 * b + 512, 0:keys]
        dprob = dot_nt(dos, VD[g, 0:keys])
        ds = probs * (dprob - jnp.sum(probs * dprob, axis=-1, keepdims=True))
        low = ds.astype(BF)
        DQ[g, rows] = unstack(dot(low, KD[g, 0:keys])) * HD**-0.5
        dk = dot_tn(low, qs)
        dv = dot_tn(probs.astype(BF), dos)
        if b == 1:
            DK[g] = dk
            DV[g] = dv
        else:
            DK[g, 0:keys] = DK[g, 0:keys] + dk
            DV[g, 0:keys] = DV[g, 0:keys] + dv

    attend_back(0, 1)
    attend_back(0, 0)
    for c in range(2, CHUNKS):
        rs3(c)
    attend_back(1, 1)
    attend_back(1, 0)
    rs4(1)

    def raw_grads(i, carry):
        rows = pl.ds(pl.multiple_of(i * 256, 256), 256)
        dks = DK[:, rows]
        dvs = DV[:, rows]
        dk = jnp.where(left_head, dks[0] + pltpu.roll(dks[0], 64, 1), dks[1] + pltpu.roll(dks[1], 64, 1))
        dv = jnp.where(left_head, dvs[0] + pltpu.roll(dvs[0], 64, 1), dvs[1] + pltpu.roll(dvs[1], 64, 1))
        DQKV[rows, 384:512] = dv.astype(BF)
        sums = []
        for g in range(3):
            e = rope_back(DQ[g, rows] if g < 2 else dk, rows)
            n = NQ[g, rows]
            sums.append(jnp.sum(e * n, axis=0, keepdims=True))
            eg = e * (q_gain if g < 2 else k_gain)
            DQKV[rows, 128 * g : 128 * g + 128] = (
                RQ[g, rows] * (eg - n * head_mean(eg * n))
            ).astype(BF)
        return carry[0] + sums[0] + sums[1], carry[1] + sums[2]

    zero = jnp.zeros((1, 128), F32)
    sum_q, sum_k = lax.fori_loop(0, 2, raw_grads, (zero, zero))
    GV[0, pl.ds(t, 1), :, 2048:2176] = sum_q.reshape(1, 1, 128)
    GV[0, pl.ds(t, 1), :, 2176:2304] = sum_k.reshape(1, 1, 128)

    G0 = Gs[0]

    def attn_grads(i, carry):
        rows = pl.ds(pl.multiple_of(i * 256, 256), 256)
        zs = pl.ds(2 * (i % 2), 2)
        G0[i // 2, zs, :, :, 0:512] = dot(A1T[rows], DQKV[...]).astype(BF).reshape(2, 4, 32, 512)
        return carry

    def out_grads():
        G0[:, :, :, :, 512:768] = (
            dot_tn(GX[...].reshape(512, D), O[...]).astype(BF).reshape(2, 4, 4, 32, 256)
        )

    out_grads()
    lax.fori_loop(0, 4, attn_grads, 0)
    rs1(0)

    def da1_part(b):
        rows = pl.ds(pl.multiple_of(b * 128, 128), 128)
        return dot_nt(DQKV[rows], W0[:, :, :, :, 0:512].reshape(D, 512)).astype(BF)

    da1_copies = sum_start(3, da1_part)
    for c in range(2, CHUNKS):
        rs4(c)
    da1_last = sum_mid(3, da1_copies)
    rs2(0)
    for c in range(1, CHUNKS):
        rs5(c)
    out[...] = (X2[...] + sum_end(2, y_copies, y_last)).astype(BF)
    da1 = sum_end(3, da1_copies, da1_last)
    n1, r1 = rms(tok[...].astype(F32))
    GV[0, pl.ds(t, 1), :, 0:1024] = jnp.sum(da1 * n1, axis=0, keepdims=True).reshape(1, 1, D)
    mine = GV.at[0, t]
    g_copies = [send(mine, mine, device) for device in (d_s, d_o, d_d)]
    h = da1 * na[...]
    gtok[...] = DX2[...] + r1 * (h - n1 * jnp.mean(h * n1, axis=-1, keepdims=True))
    rs3(0)

    def gain_stage(stage, copies, count, place, devices):
        for copy in copies:
            copy.wait_recv()
        total = GV[stage, 0]
        for i in range(1, count):
            total = total + GV[stage, i]
        GV[stage + 1, pl.ds(place, 1)] = total.reshape(1, 1, GAINS)
        v = GV.at[stage + 1, place]
        return [send(v, v, device) for device in devices]

    g_copies = gain_stage(0, g_copies, 4, x, (d_x,))
    rs4(0)
    g_copies = gain_stage(1, g_copies, 2, z, (d_zl, d_zr, d_zo))
    for c in range(1, CHUNKS):
        rs6(c)
    rs5(0)
    g_copies = gain_stage(2, g_copies, 4, y, (d_yl, d_yr, d_yo))
    rs6(0)
    for copy in g_copies:
        copy.wait_recv()
    total = GV[3, 0]
    for i in range(1, 4):
        total = total + GV[3, i]
    turned = pltpu.roll(total[:, 2048:2304], 192, 1) + total[:, 2048:2304]
    gains[:, 0:2048] = total[:, 0:2048]
    gains[:, 2048:2304] = turned

    for copy in started:
        copy.wait_send()


def on_device(
    tokens, seq_lens, norm_attn, w_query, w_key, w_value, w_out, query_gain, key_gain,
    norm_ffn, w_gate, w_up, w_down, cotangent,
):
    freq = np.exp(-math.log(THETA) * 2.0 * np.arange(HD // 2, dtype=np.float64) / HD)
    freq = jnp.asarray(np.tile(freq.astype(np.float32), 4)[None, :])
    shape = jax.ShapeDtypeStruct
    vmem = pl.BlockSpec(memory_space=pltpu.VMEM)
    outs = (
        shape((128, D), BF),
        shape((128, D), F32),
        shape((32, 256), F32),
        shape((32, 128), F32),
        shape((32, 128), F32),
        shape((32, 256), F32),
        shape((32, FFL), F32),
        shape((32, FFL), F32),
        shape((32, FFL), F32),
        shape((1, GAINS), F32),
    )
    V = pltpu.VMEM
    scratch = [
        [V((2, 4, 4, 32, w), BF) for w in WIDTHS],
        [V((2, 4, 4, 32, w), BF) for w in WIDTHS],
        [V((2, 2, 4, 16, w), BF) for w in WIDTHS],
        [V((2, 2, 2, 4, 16, w), BF) for w in WIDTHS],
        [V((2, 2, 16, w), BF) for w in WIDTHS],
        [V((2, 2, 2, 16, w), BF) for w in WIDTHS],
        [V((32, w), BF) for w in WIDTHS],
        V((4, 128, D), BF),
        V((4, 128, D), BF),
        V((4, 128, D), BF),
        V((4, 128, D), BF),
        V((D, 512), BF),
        V((D, 512), BF),
        V((D, 512), BF),
        V((4, 4, 128, D), BF),
        V((4, 2, 128, D), BF),
        V((4, 128, D), BF),
        V((128, D), F32),
        V((128, D), F32),
        V((512, 128), F32),
        V((512, 128), F32),
        V((512, 512), F32),
        V((3, 512, 128), F32),
        V((3, 512, 128), F32),
        V((2, 512, 128), BF),
        V((2, 512, 128), BF),
        V((2, 512, 128), BF),
        V((2, 1024, 512), F32),
        V((512, 256), BF),
        V((512, 256), BF),
        V((2, 512, 128), F32),
        V((2, 512, 128), F32),
        V((2, 512, 128), F32),
        V((512, 512), BF),
        V((512, FFL), BF),
        V((512, FFL), BF),
        V((512, FFL), BF),
        V((512, D), F32),
        V((4, 4, 1, GAINS), F32),
        pltpu.SemaphoreType.DMA((NSEM,)),
        pltpu.SemaphoreType.DMA((NSEM,)),
    ]
    r = pl.pallas_call(
        kernel,
        out_shape=outs,
        in_specs=[pl.BlockSpec(memory_space=pltpu.SMEM)] + [vmem] * 14,
        out_specs=[vmem] * len(outs),
        scratch_shapes=scratch,
        compiler_params=pltpu.CompilerParams(
            collective_id=0, has_side_effects=True, vmem_limit_bytes=63 * 2**20
        ),
        name="layer",
    )(
        seq_lens, tokens, cotangent, w_query, w_key, w_value, w_out.T, w_gate, w_up, w_down.T,
        norm_attn[None], norm_ffn[None], query_gain[None], key_gain[None], freq,
    )
    out, gtok, gq, gk, gv, go, gg, gu, gd, gains = r
    gains = gains[0]
    return (
        out, gtok, gains[0:1024], gq, gk, gv, go.T, gains[2048:2112], gains[2176:2240],
        gains[1024:2048], gg, gu, gd.T,
    )


def solution(mesh):
    rows = P(("dp", "tensor"), None)
    split, across, full = P("dp", "tensor"), P("tensor", "dp"), P()
    return jax.shard_map(
        on_device,
        mesh=mesh,
        in_specs=(
            rows, P("dp", None), full, split, split, split, across, full, full, full,
            split, split, across, rows,
        ),
        out_specs=(
            rows, rows, full, split, split, split, across, full, full, full, split, split, across,
        ),
        check_vma=False,
    )
```

```python
import functools
import math

import jax
import jax.numpy as jnp
import numpy as np
from jax import lax
from jax.experimental import pallas as pl
from jax.experimental.pallas import tpu as pltpu
from jax.sharding import PartitionSpec as P

MESH = pl.DeviceIdType.MESH
BF = jnp.bfloat16
F32 = jnp.float32

D = 1024
HD = 64
FF_PARTS = (256, 512, 384)
FF_OFF = tuple(int(v) for v in np.cumsum((0,) + FF_PARTS)[:-1])
WIDTHS = (768,) + tuple(3 * c for c in FF_PARTS)
CHUNKS = len(WIDTHS)
OUT = CHUNKS
SUMS = (512,) + WIDTHS[1:] + (256,)
FFL = sum(FF_PARTS)
EPS = 1e-05
THETA = 1000000.0
GAINS = 2304
NSEM = 17 * CHUNKS + 17 * len(SUMS) + 50

LO = pl.ds(0, 16)
HI = pl.ds(16, 16)


def dot(a, b):
    return jnp.dot(a, b, preferred_element_type=F32)


def dot_nt(a, b):
    return lax.dot_general(a, b, (((1,), (1,)), ((), ())), preferred_element_type=F32)


def dot_tn(a, b):
    return lax.dot_general(a, b, (((0,), (0,)), ((), ())), preferred_element_type=F32)


def rms(v):
    inverse = lax.rsqrt(jnp.mean(v * v, axis=-1, keepdims=True) + EPS)
    return v * inverse, inverse


def kernel(
    lens, tok, cot, wq, wk, wv, wo, wg, wu, wd, na, nf, qg, kg, fr,
    out, gtok, gq_w, gk_w, gv_w, go_w, gg_w, gu_w, gd_w, gna, gnf, gqg, gkg,
    Ws, Gs, RA, RB, RC, RD, RE,
    A1, A2, GO, GX, A1T, A2T, GOT,
    PB, T1, T2, X2, DX2,
    COS, SIN, BIAS, NQ, RQ, QS, KD, VD, PR, O, DO, DQ, DK, DV, DQKV,
    HID, DG, DU, DA, GVA, GVB,
    ssem, rsem,
):
    me = lax.axis_index("dp")
    t = lax.axis_index("tensor")
    x = me // 16
    z = (me // 4) % 4
    y = me % 4
    xo = (x + 1) % 2
    zl, zr, zo = (z + 3) % 4, (z + 1) % 4, (z + 2) % 4
    yl, yr, yo = (y + 3) % 4, (y + 1) % 4, (y + 2) % 4
    ts = t + 1 - 2 * (t % 2)
    to = (t + 2) % 4
    td = (ts + 2) % 4

    def dp(xx, zz, yy):
        return (xx * 16 + zz * 4 + yy, t)

    d_x = dp(xo, z, y)
    d_zl, d_zr, d_zo = dp(x, zl, y), dp(x, zr, y), dp(x, zo, y)
    d_yl, d_yr, d_yo = dp(x, z, yl), dp(x, z, yr), dp(x, z, yo)
    d_s, d_o, d_d = (me, ts), (me, to), (me, td)
    ring_z, ring_y = (d_zr, d_zl, d_zo), (d_yr, d_yl, d_yo)
    near = (d_s, d_o, d_d, d_x) + tuple((d_x[0], other) for other in (ts, to, td))
    plane = tuple(
        dp(x, (z + i) % 4, (y + j) % 4) for i in range(4) for j in range(4) if i or j
    )
    partners = near + plane

    slot = x * 4 + t
    started = []

    def send(src, dst, device):
        index = len(started)
        copy = pltpu.make_async_remote_copy(
            src_ref=src,
            dst_ref=dst,
            send_sem=ssem.at[index],
            recv_sem=rsem.at[index],
            device_id=device,
            device_id_type=MESH,
        )
        copy.start()
        started.append(copy)
        return copy

    ag = {}

    def ag0(c):
        W = Ws[c]
        ag[c, 0] = send(W.at[x, z, y], W.at[x, z, y], d_x)

    def ag1(c):
        W = Ws[c]
        ag[c, 0].wait_recv()
        a, b = W.at[:, z, y, LO], W.at[:, z, y, HI]
        ag[c, 1] = (send(a, a, d_zr), send(a, a, d_zl), send(b, b, d_yr), send(b, b, d_yl))

    def ag2(c):
        W, r = Ws[c], ag[c, 1]
        r[0].wait_recv()
        v = W.at[0, zl, y, LO]
        f0 = send(v, v, d_zr)
        r[2].wait_recv()
        v = W.at[0, z, yl, HI]
        f2 = send(v, v, d_yr)
        r[1].wait_recv()
        v = W.at[1, zr, y, LO]
        f1 = send(v, v, d_zl)
        r[3].wait_recv()
        v = W.at[1, z, yr, HI]
        f3 = send(v, v, d_yl)
        ag[c, 2] = (f0, f1, f2, f3)

    def ag3(c):
        W, r = Ws[c], ag[c, 2]
        r[0].wait_recv()
        r[1].wait_recv()
        a = W.at[:, :, y, LO]
        f0, f1 = send(a, a, d_yr), send(a, a, d_yl)
        r[2].wait_recv()
        r[3].wait_recv()
        b = W.at[:, z, :, HI]
        ag[c, 3] = (f0, f1, send(b, b, d_zr), send(b, b, d_zl))

    def ag4(c):
        W, r = Ws[c], ag[c, 3]
        r[0].wait_recv()
        v = W.at[0, :, yl, LO]
        f0 = send(v, v, d_yr)
        r[2].wait_recv()
        v = W.at[0, zl, :, HI]
        f2 = send(v, v, d_zr)
        r[1].wait_recv()
        v = W.at[1, :, yr, LO]
        f1 = send(v, v, d_yl)
        r[3].wait_recv()
        v = W.at[1, zr, :, HI]
        f3 = send(v, v, d_zl)
        ag[c, 4] = (f0, f1, f2, f3)

    def ag5(c):
        for copy in ag[c, 4]:
            copy.wait_recv()

    def ag1_direct(c):
        W = Ws[c]
        ag[c, 0].wait_recv()
        a, b = W.at[:, z, y, LO], W.at[:, z, y, HI]
        ag[c, 1] = [send(a, a, d) for d in ring_z], [send(b, b, d) for d in ring_y]

    def ag2_direct(c):
        W = Ws[c]
        for copy in ag[c, 1][0]:
            copy.wait_recv()
        a = W.at[:, :, y, LO]
        first = [send(a, a, d) for d in ring_y]
        for copy in ag[c, 1][1]:
            copy.wait_recv()
        b = W.at[:, z, :, HI]
        ag[c, 4] = first + [send(b, b, d) for d in ring_z]

    rs = {}

    def add(ref, index, *others):
        total = ref[index].astype(F32)
        for other in others:
            total = total + other.astype(F32).reshape(total.shape)
        ref[index] = total.astype(BF)

    lo, hi = slice(0, 16), slice(16, 32)
    every = slice(None)

    def one(i):
        return pl.ds(i, 1)

    def rs1(c):
        G, ra = Gs[c], RA[c]
        rs[c, 1] = (
            send(G.at[0, :, yo, LO], ra.at[0, 0], d_yr),
            send(G.at[1, :, yo, LO], ra.at[0, 1], d_yl),
            send(G.at[0, zo, :, HI], ra.at[1, 0], d_zr),
            send(G.at[1, zo, :, HI], ra.at[1, 1], d_zl),
        )

    def rs2(c):
        G, ra, rb, r = Gs[c], RA[c], RB[c], rs[c, 1]
        r[0].wait_recv()
        add(G, (0, every, one(yr), lo), ra[0, 0])
        f0 = send(G.at[:, :, yr, LO], rb.at[0, 0], d_yr)
        r[2].wait_recv()
        add(G, (0, one(zr), every, hi), ra[1, 0])
        f2 = send(G.at[:, zr, :, HI], rb.at[1, 0], d_zr)
        r[1].wait_recv()
        add(G, (1, every, one(yl), lo), ra[0, 1])
        f1 = send(G.at[:, :, yl, LO], rb.at[0, 1], d_yl)
        r[3].wait_recv()
        add(G, (1, one(zl), every, hi), ra[1, 1])
        f3 = send(G.at[:, zl, :, HI], rb.at[1, 1], d_zl)
        rs[c, 2] = (f0, f1, f2, f3)

    def rs3(c):
        G, rb, rc, r = Gs[c], RB[c], RC[c], rs[c, 2]
        r[0].wait_recv()
        r[1].wait_recv()
        add(G, (every, every, one(y), lo), rb[0, 0], rb[0, 1])
        f0 = send(G.at[0, zo, y, LO], rc.at[0, 0], d_zr)
        f1 = send(G.at[1, zo, y, LO], rc.at[0, 1], d_zl)
        r[2].wait_recv()
        r[3].wait_recv()
        add(G, (every, one(z), every, hi), rb[1, 0], rb[1, 1])
        f2 = send(G.at[0, z, yo, HI], rc.at[1, 0], d_yr)
        f3 = send(G.at[1, z, yo, HI], rc.at[1, 1], d_yl)
        rs[c, 3] = (f0, f1, f2, f3)

    def rs4(c):
        G, rc, rd, r = Gs[c], RC[c], RD[c], rs[c, 3]
        r[0].wait_recv()
        add(G, (0, one(zr), one(y), lo), rc[0, 0])
        f0 = send(G.at[:, zr, y, LO], rd.at[0, 0], d_zr)
        r[2].wait_recv()
        add(G, (0, one(z), one(yr), hi), rc[1, 0])
        f2 = send(G.at[:, z, yr, HI], rd.at[1, 0], d_yr)
        r[1].wait_recv()
        add(G, (1, one(zl), one(y), lo), rc[0, 1])
        f1 = send(G.at[:, zl, y, LO], rd.at[0, 1], d_zl)
        r[3].wait_recv()
        add(G, (1, one(z), one(yl), hi), rc[1, 1])
        f3 = send(G.at[:, z, yl, HI], rd.at[1, 1], d_yl)
        rs[c, 4] = (f0, f1, f2, f3)

    def rs5(c):
        G, rd, r = Gs[c], RD[c], rs[c, 4]
        for copy in r:
            copy.wait_recv()
        add(G, (every, one(z), one(y), lo), rd[0, 0], rd[0, 1])
        add(G, (every, one(z), one(y), hi), rd[1, 0], rd[1, 1])
        rs[c, 5] = send(G.at[xo, z, y], RE[c], d_x)

    def rs6(c):
        rs[c, 5].wait_recv()
        total = Gs[c][x, z, y].astype(F32) + RE[c][...].astype(F32)
        if c == 0:
            gq_w[...] = total[:, 0:256]
            gk_w[...] = total[:, 256:384]
            gv_w[...] = total[:, 384:512]
        elif c == OUT:
            go_w[...] = total
        else:
            w, o = FF_PARTS[c - 1], FF_OFF[c - 1]
            gg_w[:, o : o + w] = total[:, 0:w]
            gu_w[:, o : o + w] = total[:, w : 2 * w]
            gd_w[:, o : o + w] = total[:, 2 * w : 3 * w]

    def rs1_direct(c):
        G, rb = Gs[c], RB[c]
        a = [send(G.at[:, :, i, LO], rb.at[0, k], d) for k, (i, d) in enumerate(zip((yr, yl, yo), ring_y))]
        b = [send(G.at[:, i, :, HI], rb.at[1, k], d) for k, (i, d) in enumerate(zip((zr, zl, zo), ring_z))]
        rs[c, 2] = a, b

    def rs3_direct(c):
        G, rb, rd, (a, b) = Gs[c], RB[c], RD[c], rs[c, 2]
        for copy in a:
            copy.wait_recv()
        add(G, (every, every, one(y), lo), rb[0, 0], rb[0, 1], rb[0, 2])
        a = [send(G.at[:, i, y, LO], rd.at[0, k], d) for k, (i, d) in enumerate(zip((zr, zl, zo), ring_z))]
        for copy in b:
            copy.wait_recv()
        add(G, (every, one(z), every, hi), rb[1, 0], rb[1, 1], rb[1, 2])
        b = [send(G.at[:, z, i, HI], rd.at[1, k], d) for k, (i, d) in enumerate(zip((yr, yl, yo), ring_y))]
        rs[c, 4] = a + b

    def rs5_direct(c):
        G, rd = Gs[c], RD[c]
        for copy in rs[c, 4]:
            copy.wait_recv()
        add(G, (every, one(z), one(y), lo), rd[0, 0], rd[0, 1], rd[0, 2])
        add(G, (every, one(z), one(y), hi), rd[1, 0], rd[1, 1], rd[1, 2])
        rs[c, 5] = send(G.at[xo, z, y], RE[c], d_x)

    def rows_start(buf):
        v = buf.at[t]
        return send(v, v, d_o), send(v, v, d_s)

    def rows_relay(buf, pair):
        pair[0].wait_recv()
        v = buf.at[to]
        return send(v, v, d_s)

    def rows_end(pair, relay):
        pair[1].wait_recv()
        relay.wait_recv()

    def sum_far(k, part):
        PB[k, td] = part(td)
        copy = send(PB.at[k, td], T1.at[k, 1], d_s)
        PB[k, to] = part(to)
        return (copy,)

    def sum_near(k, part):
        PB[k, ts] = part(ts)
        copy = send(PB.at[k, ts], T1.at[k, 0], d_s)
        PB[k, t] = part(t)
        return (copy,)

    def sum_start(k, part):
        return sum_far(k, part) + sum_near(k, part)

    def sum_mid(k, copies):
        copies[0].wait_recv()
        PB[k, to] = (PB[k, to].astype(F32) + T1[k, 1].astype(F32)).astype(BF)
        return send(PB.at[k, to], T2.at[k], d_o)

    def sum_end(k, copies, last):
        copies[1].wait_recv()
        part = PB[k, t].astype(F32) + T1[k, 0].astype(F32)
        last.wait_recv()
        return part + T2[k].astype(F32)

    barrier = pltpu.get_barrier_semaphore()
    for device in partners:
        pl.semaphore_signal(barrier, inc=1, device_id=device, device_id_type=MESH)

    W0 = Ws[0]
    W0[x, z, y, :, 0:256] = wq[...]
    W0[x, z, y, :, 256:384] = wk[...]
    W0[x, z, y, :, 384:512] = wv[...]
    W0[x, z, y, :, 512:768] = wo[...]
    for c in range(1, CHUNKS):
        w, o = FF_PARTS[c - 1], FF_OFF[c - 1]
        Ws[c][x, z, y, :, 0:w] = wg[:, o : o + w]
        Ws[c][x, z, y, :, w : 2 * w] = wu[:, o : o + w]
        Ws[c][x, z, y, :, 2 * w : 3 * w] = wd[:, o : o + w]
    n1, _ = rms(tok[...].astype(F32))
    A1[t] = (n1 * na[...]).astype(BF)
    GO[t] = cot[...]

    pl.semaphore_wait(barrier, len(partners))

    ag0(0)
    a1_pair = rows_start(A1)
    for c in range(1, CHUNKS):
        ag0(c)

    lane = lax.broadcasted_iota(jnp.int32, (1, 128), 1)
    left_head = lane < 64
    first_half = (lane % 64) < 32

    e1 = lens[0, 0]
    e2 = e1 + lens[0, 1]
    e3 = e2 + lens[0, 2]

    def begin(row):
        return jnp.where(
            row >= e3, e3, jnp.where(row >= e2, e2, jnp.where(row >= e1, e1, 0))
        )

    def fill_tables(i, carry):
        rows = pl.ds(pl.multiple_of(i * 128, 128), 128)
        row = lax.broadcasted_iota(jnp.int32, (128, 128), 0) + i * 128
        angle = (row - begin(row)).astype(F32) * fr[...]
        COS[rows] = jnp.cos(angle)
        SIN[rows] = jnp.where(first_half, -1.0, 1.0) * jnp.sin(angle)
        return carry

    def fill_bias(i, carry):
        rows = pl.ds(pl.multiple_of(i * 128, 128), 128)
        row = lax.broadcasted_iota(jnp.int32, (128, 512), 0) + i * 128
        col = lax.broadcasted_iota(jnp.int32, (128, 512), 1)
        seen = (col <= row) & (col >= begin(row))
        BIAS[rows] = jnp.where(seen, 0.0, -1e30)
        return carry

    lax.fori_loop(0, 4, fill_tables, 0)
    ag1_direct(0)
    a1_relay = rows_relay(A1, a1_pair)
    ag1(1)
    lax.fori_loop(0, 4, fill_bias, 0)
    ag2_direct(0)
    rows_end(a1_pair, a1_relay)
    ag2(1)
    for c in range(2, CHUNKS):
        ag1(c)
    A1T[...] = A1[...].reshape(512, D).T
    ag3(1)
    for c in range(2, CHUNKS):
        ag2(c)
    ag5(0)
    go_pair = rows_start(GO)
    for c in range(2, CHUNKS):
        ag3(c)

    def rope(v, rows):
        swapped = jnp.where(first_half, pltpu.roll(v, 96, 1), pltpu.roll(v, 32, 1))
        return v * COS[rows] + swapped * SIN[rows]

    def rope_back(v, rows):
        swapped = jnp.where(first_half, pltpu.roll(v, 96, 1), pltpu.roll(v, 32, 1))
        return v * COS[rows] - swapped * SIN[rows]

    hr = lax.broadcasted_iota(jnp.int32, (128, 128), 0) // 64
    hc = lax.broadcasted_iota(jnp.int32, (128, 128), 1) // 64
    mean_of = jnp.where(hr == hc, 1.0 / HD, 0.0).astype(BF)

    def head_mean(v):
        high = v.astype(BF)
        low = (v - high.astype(F32)).astype(BF)
        return dot(high, mean_of) + dot(low, mean_of)

    q_gain = jnp.concatenate([qg[...], qg[...]], axis=1)
    k_gain = jnp.concatenate([kg[...], kg[...]], axis=1)

    def qkv_block(i, carry):
        rows = pl.ds(pl.multiple_of(i * 256, 256), 256)
        raw = dot(A1[pl.ds(2 * i, 2)].reshape(256, D), W0[:, :, :, :, 0:512].reshape(D, 512))
        for g in range(3):
            v = raw[:, 128 * g : 128 * g + 128]
            inverse = lax.rsqrt(head_mean(v * v) + EPS)
            n = v * inverse
            NQ[g, rows] = n
            RQ[g, rows] = inverse
            r = rope(n * (q_gain if g < 2 else k_gain), rows)
            if g < 2:
                QS[g, rows] = (r * HD**-0.5).astype(BF)
            else:
                turned = pltpu.roll(r, 64, 1)
                KD[0, rows] = jnp.where(left_head, r, turned).astype(BF)
                KD[1, rows] = jnp.where(left_head, turned, r).astype(BF)
        v = raw[:, 384:512]
        turned = pltpu.roll(v, 64, 1)
        VD[0, rows] = jnp.where(left_head, v, turned).astype(BF)
        VD[1, rows] = jnp.where(left_head, turned, v).astype(BF)
        return carry

    lax.fori_loop(0, 2, qkv_block, 0)

    def stack(v):
        none = jnp.zeros_like(v)
        return jnp.concatenate(
            [jnp.where(left_head, v, none), jnp.where(left_head, none, v)], axis=0
        )

    def unstack(v):
        half = v.shape[0] // 2
        return jnp.where(left_head, v[:half], v[half:])

    def attend(g, i):
        rows = pl.ds(pl.multiple_of(i * 256, 256), 256)
        scores = dot_nt(stack(QS[g, rows]), KD[g])
        bias = BIAS[rows]
        scores = scores + jnp.concatenate([bias, bias], axis=0)
        expo = jnp.exp(scores - jnp.max(scores, axis=-1, keepdims=True))
        probs = expo * (1.0 / jnp.sum(expo, axis=-1, keepdims=True))
        PR[g, pl.ds(pl.multiple_of(i * 512, 512), 512)] = probs
        O[rows, 128 * g : 128 * g + 128] = unstack(dot(probs.astype(BF), VD[g])).astype(BF)

    here = t // 2
    there = 1 - here

    def out_part(b):
        rows = pl.ds(pl.multiple_of(b * 128, 128), 128)
        return dot_nt(O[rows], W0[:, :, :, :, 512:768].reshape(D, 256)).astype(BF)

    attend(0, there)
    attend(1, there)
    at_copies = sum_far(0, out_part)
    ag4(1)
    go_relay = rows_relay(GO, go_pair)
    attend(0, here)
    at_last = sum_mid(0, at_copies)
    attend(1, here)
    at_copies += sum_near(0, out_part)
    rows_end(go_pair, go_relay)
    GOT[...] = GO[...].reshape(512, D).T
    ag4(2)
    x2 = tok[...].astype(F32) + sum_end(0, at_copies, at_last)
    X2[...] = x2
    n2, _ = rms(x2)
    A2[t] = (n2 * nf[...]).astype(BF)
    a2_pair = rows_start(A2)
    ag5(1)
    for c in range(3, CHUNKS):
        ag4(c)

    def ffn_chunk(c, i):
        W = Ws[c]
        w, o = FF_PARTS[c - 1], FF_OFF[c - 1]
        cols = slice(o, o + w)

        rows = pl.ds(pl.multiple_of(i * 256, 256), 256)
        a = A2[pl.ds(2 * i, 2)].reshape(256, D)
        g = GO[pl.ds(2 * i, 2)].reshape(256, D)
        gate = dot(a, W[:, :, :, :, 0:w].reshape(D, w))
        up = dot(a, W[:, :, :, :, w : 2 * w].reshape(D, w))
        dhid = dot(g, W[:, :, :, :, 2 * w : 3 * w].reshape(D, w))
        sigma = jax.nn.sigmoid(gate)
        swish = gate * sigma
        HID[rows, cols] = (swish * up).astype(BF)
        dgate = (dhid * up * sigma * (1.0 + gate * (1.0 - sigma))).astype(BF)
        dup = (dhid * swish).astype(BF)
        DG[rows, cols] = dgate
        DU[rows, cols] = dup
        part = dot_nt(dgate, W[:, :, :, :, 0:w].reshape(D, w)) + dot_nt(
            dup, W[:, :, :, :, w : 2 * w].reshape(D, w)
        )
        if c == 1:
            DA[rows] = part
        else:
            DA[rows] = DA[rows] + part

    def ffn_grads(c):
        G = Gs[c]
        w, o = FF_PARTS[c - 1], FF_OFF[c - 1]
        cols = slice(o, o + w)

        def block(i, carry):
            rows = pl.ds(pl.multiple_of(i * 256, 256), 256)
            zs = pl.ds(2 * (i % 2), 2)
            a, g = A2T[rows], GOT[rows]
            G[i // 2, zs, :, :, 0:w] = dot(a, DG[:, cols]).astype(BF).reshape(2, 4, 32, w)
            G[i // 2, zs, :, :, w : 2 * w] = dot(a, DU[:, cols]).astype(BF).reshape(2, 4, 32, w)
            G[i // 2, zs, :, :, 2 * w : 3 * w] = dot(g, HID[:, cols]).astype(BF).reshape(2, 4, 32, w)
            return carry

        lax.fori_loop(0, 4, block, 0)

    def da2_part(b):
        rows = pl.ds(pl.multiple_of(b * 128, 128), 128)
        return DA[rows].astype(BF)

    a2_pair[1].wait_recv()
    ffn_chunk(1, here)
    a2_relay = rows_relay(A2, a2_pair)
    ag5(2)
    ffn_chunk(2, here)
    a2_relay.wait_recv()
    A2T[...] = A2[...].reshape(512, D).T
    ffn_chunk(1, there)
    ffn_grads(1)
    rs1(1)
    for c in range(2, CHUNKS):
        if c > 2:
            ag5(c)
        ffn_chunk(c, there)
        if c + 1 == CHUNKS:
            da2_copies = sum_far(1, da2_part)
        if c > 2:
            ffn_chunk(c, here)
    da2_copies += sum_near(1, da2_part)
    da2_last = sum_mid(1, da2_copies)
    rs2(1)
    for c in range(2, CHUNKS):
        ffn_grads(c)
        rs1(c)

    def y_part(b):
        rows = pl.ds(pl.multiple_of(b * 128, 128), 128)
        total = None
        for c in range(1, CHUNKS):
            w, o = FF_PARTS[c - 1], FF_OFF[c - 1]
            part = dot_nt(HID[rows, o : o + w], Ws[c][:, :, :, :, 2 * w : 3 * w].reshape(D, w))
            total = part if total is None else total + part
        return total.astype(BF)

    da2 = sum_end(1, da2_copies, da2_last)
    n2, r2 = rms(X2[...])
    GVA[pl.ds(slot, 1), :, 1024:2048] = jnp.sum(da2 * n2, axis=0, keepdims=True).reshape(1, 1, D)
    h = da2 * nf[...]
    dx2 = cot[...].astype(F32) + r2 * (h - n2 * jnp.mean(h * n2, axis=-1, keepdims=True))
    DX2[...] = dx2
    GX[t] = dx2.astype(BF)
    gx_pair = rows_start(GX)
    rs2(2)
    y_copies = sum_far(2, y_part)

    def do_block(i):
        rows = pl.ds(pl.multiple_of(i * 256, 256), 256)
        g = GX[pl.ds(2 * i, 2)].reshape(256, D)
        DO[rows] = dot(g, W0[:, :, :, :, 512:768].reshape(D, 256)).astype(BF)

    def attend_back(g, i, first):
        rows = pl.ds(pl.multiple_of(i * 256, 256), 256)
        qs = stack(QS[g, rows])
        dos = stack(DO[rows, 128 * g : 128 * g + 128])
        probs = PR[g, pl.ds(pl.multiple_of(i * 512, 512), 512)]
        dprob = dot_nt(dos, VD[g])
        ds = probs * (dprob - jnp.sum(probs * dprob, axis=-1, keepdims=True))
        low = ds.astype(BF)
        DQ[g, rows] = unstack(dot(low, KD[g])) * HD**-0.5
        dk = dot_tn(low, qs)
        dv = dot_tn(probs.astype(BF), dos)
        if first:
            DK[g] = dk
            DV[g] = dv
        else:
            DK[g] = DK[g] + dk
            DV[g] = DV[g] + dv

    gx_pair[1].wait_recv()
    do_block(here)
    attend_back(0, here, True)
    gx_relay = rows_relay(GX, gx_pair)
    attend_back(1, here, True)
    y_copies += sum_near(2, y_part)
    for c in range(3, CHUNKS):
        rs2(c)
    gx_relay.wait_recv()
    do_block(there)
    Gs[OUT][...] = dot_tn(GX[...].reshape(512, D), O[...]).astype(BF).reshape(2, 4, 4, 32, 256)
    rs1_direct(OUT)
    attend_back(0, there, False)
    rs3(1)
    attend_back(1, there, False)
    rs3(2)

    def raw_grads(i, carry):
        rows = pl.ds(pl.multiple_of(i * 256, 256), 256)
        dks = DK[:, rows]
        dvs = DV[:, rows]
        dk = jnp.where(left_head, dks[0] + pltpu.roll(dks[0], 64, 1), dks[1] + pltpu.roll(dks[1], 64, 1))
        dv = jnp.where(left_head, dvs[0] + pltpu.roll(dvs[0], 64, 1), dvs[1] + pltpu.roll(dvs[1], 64, 1))
        DQKV[rows, 384:512] = dv.astype(BF)
        sums = []
        for g in range(3):
            e = rope_back(DQ[g, rows] if g < 2 else dk, rows)
            n = NQ[g, rows]
            sums.append(jnp.sum(e * n, axis=0, keepdims=True))
            eg = e * (q_gain if g < 2 else k_gain)
            DQKV[rows, 128 * g : 128 * g + 128] = (
                RQ[g, rows] * (eg - n * head_mean(eg * n))
            ).astype(BF)
        return carry[0] + sums[0] + sums[1], carry[1] + sums[2]

    zero = jnp.zeros((1, 128), F32)
    sum_q, sum_k = lax.fori_loop(0, 2, raw_grads, (zero, zero))
    GVA[pl.ds(slot, 1), :, 2048:2176] = sum_q.reshape(1, 1, 128)
    GVA[pl.ds(slot, 1), :, 2176:2304] = sum_k.reshape(1, 1, 128)

    G0 = Gs[0]

    def attn_grads(i, carry):
        rows = pl.ds(pl.multiple_of(i * 256, 256), 256)
        zs = pl.ds(2 * (i % 2), 2)
        G0[i // 2, zs, :, :, 0:512] = dot(A1T[rows], DQKV[...]).astype(BF).reshape(2, 4, 32, 512)
        return carry

    def da1_part(b):
        rows = pl.ds(pl.multiple_of(b * 128, 128), 128)
        return dot_nt(DQKV[rows], W0[:, :, :, :, 0:512].reshape(D, 512)).astype(BF)

    da1_copies = sum_start(3, da1_part)
    lax.fori_loop(0, 4, attn_grads, 0)
    rs1_direct(0)
    da1_last = sum_mid(3, da1_copies)
    rs3_direct(OUT)
    rs4(1)
    for c in range(3, CHUNKS):
        rs3(c)
    y_last = sum_mid(2, y_copies)
    rs4(2)
    rs5(1)
    rs3_direct(0)
    rs5_direct(OUT)
    for c in range(3, CHUNKS):
        rs4(c)
    rs5(2)
    da1 = sum_end(3, da1_copies, da1_last)
    n1, r1 = rms(tok[...].astype(F32))
    GVA[pl.ds(slot, 1), :, 0:1024] = jnp.sum(da1 * n1, axis=0, keepdims=True).reshape(1, 1, D)
    mine = GVA.at[slot]
    g_copies = [send(mine, mine, device) for device in near]
    h = da1 * na[...]
    gtok[...] = DX2[...] + r1 * (h - n1 * jnp.mean(h * n1, axis=-1, keepdims=True))
    rs5_direct(0)

    def total_of(ref, count, copies):
        for copy in copies:
            copy.wait_recv()
        total = ref[0]
        for i in range(1, count):
            total = total + ref[i]
        return total

    GVB[pl.ds(z * 4 + y, 1)] = total_of(GVA, 8, g_copies).reshape(1, 1, GAINS)
    mine = GVB.at[z * 4 + y]
    g_copies = [send(mine, mine, device) for device in plane]
    for c in range(3, CHUNKS):
        rs5(c)
    out[...] = (X2[...] + sum_end(2, y_copies, y_last)).astype(BF)
    for c in range(1, CHUNKS):
        rs6(c)
    rs6(OUT)
    rs6(0)
    total = total_of(GVB, 16, g_copies)
    turned = pltpu.roll(total[:, 2048:2304], 192, 1) + total[:, 2048:2304]
    gna[...] = total[:, 0:1024]
    gnf[...] = total[:, 1024:2048]
    gqg[...] = turned[:, 0:64]
    gkg[...] = turned[:, 128:192]

    for copy in started:
        copy.wait_send()


def hand_on(*refs):
    count = len(refs) // 2
    sems = refs[-1]
    copies = [
        pltpu.make_async_copy(refs[i], refs[count + i], sems.at[i]) for i in range(count)
    ]
    for copy in copies:
        copy.start()
    for copy in copies:
        copy.wait()


def on_device(
    tokens, seq_lens, norm_attn, w_query, w_key, w_value, w_out, query_gain, key_gain,
    norm_ffn, w_gate, w_up, w_down, cotangent,
):
    freq = np.exp(-math.log(THETA) * 2.0 * np.arange(HD // 2, dtype=np.float64) / HD)
    freq = jnp.asarray(np.tile(freq.astype(np.float32), 4)[None, :])
    shape = jax.ShapeDtypeStruct
    vmem = pl.BlockSpec(memory_space=pltpu.VMEM)
    outs = (
        shape((128, D), BF),
        shape((128, D), F32),
        shape((32, 256), F32),
        shape((32, 128), F32),
        shape((32, 128), F32),
        shape((32, 256), F32),
        shape((32, FFL), F32),
        shape((32, FFL), F32),
        shape((32, FFL), F32),
        shape((1, D), F32),
        shape((1, D), F32),
        shape((1, HD), F32),
        shape((1, HD), F32),
    )
    V = pltpu.VMEM
    scratch = [
        [V((2, 4, 4, 32, w), BF) for w in WIDTHS],
        [V((2, 4, 4, 32, w), BF) for w in SUMS],
        [V((2, 2, 4, 16, w) if 0 < i < OUT else (16, 128), BF) for i, w in enumerate(SUMS)],
        [V((2, 2 if 0 < i < OUT else 3, 2, 4, 16, w), BF) for i, w in enumerate(SUMS)],
        [V((2, 2, 16, w) if 0 < i < OUT else (16, 128), BF) for i, w in enumerate(SUMS)],
        [V((2, 2 if 0 < i < OUT else 3, 2, 16, w), BF) for i, w in enumerate(SUMS)],
        [V((32, w), BF) for w in SUMS],
        V((4, 128, D), BF),
        V((4, 128, D), BF),
        V((4, 128, D), BF),
        V((4, 128, D), BF),
        V((D, 512), BF),
        V((D, 512), BF),
        V((D, 512), BF),
        V((4, 4, 128, D), BF),
        V((4, 2, 128, D), BF),
        V((4, 128, D), BF),
        V((128, D), F32),
        V((128, D), F32),
        V((512, 128), F32),
        V((512, 128), F32),
        V((512, 512), F32),
        V((3, 512, 128), F32),
        V((3, 512, 128), F32),
        V((2, 512, 128), BF),
        V((2, 512, 128), BF),
        V((2, 512, 128), BF),
        V((2, 1024, 512), F32),
        V((512, 256), BF),
        V((512, 256), BF),
        V((2, 512, 128), F32),
        V((2, 512, 128), F32),
        V((2, 512, 128), F32),
        V((512, 512), BF),
        V((512, FFL), BF),
        V((512, FFL), BF),
        V((512, FFL), BF),
        V((512, D), F32),
        V((8, 1, GAINS), F32),
        V((16, 1, GAINS), F32),
        pltpu.SemaphoreType.DMA((NSEM,)),
        pltpu.SemaphoreType.DMA((NSEM,)),
    ]
    r = pl.pallas_call(
        kernel,
        out_shape=outs,
        in_specs=[pl.BlockSpec(memory_space=pltpu.SMEM)] + [vmem] * 14,
        out_specs=[vmem] * len(outs),
        scratch_shapes=scratch,
        compiler_params=pltpu.CompilerParams(
            collective_id=0, has_side_effects=True, vmem_limit_bytes=63 * 2**20
        ),
        name="layer",
    )(
        seq_lens, tokens, cotangent, w_query, w_key, w_value, w_out.T, w_gate, w_up, w_down.T,
        norm_attn[None], norm_ffn[None], query_gain[None], key_gain[None], freq,
    )
    anywhere = pl.BlockSpec(memory_space=pl.ANY)
    r = pl.pallas_call(
        hand_on,
        out_shape=outs,
        in_specs=[vmem] * len(outs),
        out_specs=[anywhere] * len(outs),
        scratch_shapes=[pltpu.SemaphoreType.DMA((len(outs),))],
        name="hand_on",
    )(*r)
    out, gtok, gq, gk, gv, go, gg, gu, gd, gna, gnf, gqg, gkg = r
    return (out, gtok, gna[0], gq, gk, gv, go.T, gqg[0], gkg[0], gnf[0], gg, gu, gd.T)


def solution(mesh):
    rows = P(("dp", "tensor"), None)
    split, across, full = P("dp", "tensor"), P("tensor", "dp"), P()
    return jax.shard_map(
        on_device,
        mesh=mesh,
        in_specs=(
            rows, P("dp", None), full, split, split, split, across, full, full, full,
            split, split, across, rows,
        ),
        out_specs=(
            rows, rows, full, split, split, split, across, full, full, full, split, split, across,
        ),
        check_vma=False,
    )
```

```python
import functools
import math

import jax
import jax.numpy as jnp
import numpy as np
from jax import lax
from jax.experimental import pallas as pl
from jax.experimental.pallas import tpu as pltpu
from jax.sharding import PartitionSpec as P

MESH = pl.DeviceIdType.MESH
BF = jnp.bfloat16
F32 = jnp.float32

D = 1024
HD = 64
FF_PARTS = (256, 512, 384)
FF_OFF = tuple(int(v) for v in np.cumsum((0,) + FF_PARTS)[:-1])
WIDTHS = (768,) + tuple(3 * c for c in FF_PARTS)
CHUNKS = len(WIDTHS)
OUT = CHUNKS
SUMS = (512,) + WIDTHS[1:] + (256,)
FFL = sum(FF_PARTS)
EPS = 1e-05
THETA = 1000000.0
GAINS = 2304
NSEM = 17 * CHUNKS + 17 * len(SUMS) + 50

LO = pl.ds(0, 16)
HI = pl.ds(16, 16)


def dot(a, b):
    return jnp.dot(a, b, preferred_element_type=F32)


def dot_nt(a, b):
    return lax.dot_general(a, b, (((1,), (1,)), ((), ())), preferred_element_type=F32)


def dot_tn(a, b):
    return lax.dot_general(a, b, (((0,), (0,)), ((), ())), preferred_element_type=F32)


def rms(v):
    inverse = lax.rsqrt(jnp.mean(v * v, axis=-1, keepdims=True) + EPS)
    return v * inverse, inverse


def kernel(
    lens, tok, cot, wq, wk, wv, wo, wg, wu, wd, na, nf, qg, kg, fr,
    out, gtok, gq_w, gk_w, gv_w, go_w, gg_w, gu_w, gd_w, gna, gnf, gqg, gkg,
    Ws, Gs, RA, RB, RC, RD, RE,
    A1, A2, GO, GX, A1T, A2T, GOT,
    PB, T1, T2, X2, DX2,
    COS, SIN, BIAS, NQ, RQ, QS, KD, VD, PR, O, DO, DQ, DK, DV, DQKV,
    HID, DG, DU, DA, GVA, GVB,
    ssem, rsem,
):
    me = lax.axis_index("dp")
    t = lax.axis_index("tensor")
    x = me // 16
    z = (me // 4) % 4
    y = me % 4
    xo = (x + 1) % 2
    zl, zr, zo = (z + 3) % 4, (z + 1) % 4, (z + 2) % 4
    yl, yr, yo = (y + 3) % 4, (y + 1) % 4, (y + 2) % 4
    ts = t + 1 - 2 * (t % 2)
    to = (t + 2) % 4
    td = (ts + 2) % 4

    def dp(xx, zz, yy):
        return (xx * 16 + zz * 4 + yy, t)

    d_x = dp(xo, z, y)
    d_zl, d_zr, d_zo = dp(x, zl, y), dp(x, zr, y), dp(x, zo, y)
    d_yl, d_yr, d_yo = dp(x, z, yl), dp(x, z, yr), dp(x, z, yo)
    d_s, d_o, d_d = (me, ts), (me, to), (me, td)
    ring_z, ring_y = (d_zr, d_zl, d_zo), (d_yr, d_yl, d_yo)
    near = (d_s, d_o, d_d, d_x) + tuple((d_x[0], other) for other in (ts, to, td))
    plane = tuple(
        dp(x, (z + i) % 4, (y + j) % 4) for i in range(4) for j in range(4) if i or j
    )
    partners = near + plane

    slot = x * 4 + t
    started = []

    def send(src, dst, device):
        index = len(started)
        copy = pltpu.make_async_remote_copy(
            src_ref=src,
            dst_ref=dst,
            send_sem=ssem.at[index],
            recv_sem=rsem.at[index],
            device_id=device,
            device_id_type=MESH,
        )
        copy.start()
        started.append(copy)
        return copy

    ag = {}

    def ag0(c):
        W = Ws[c]
        ag[c, 0] = send(W.at[x, z, y], W.at[x, z, y], d_x)

    def ag1(c):
        W = Ws[c]
        ag[c, 0].wait_recv()
        a, b = W.at[:, z, y, LO], W.at[:, z, y, HI]
        ag[c, 1] = (send(a, a, d_zr), send(a, a, d_zl), send(b, b, d_yr), send(b, b, d_yl))

    def ag2(c):
        W, r = Ws[c], ag[c, 1]
        r[0].wait_recv()
        v = W.at[0, zl, y, LO]
        f0 = send(v, v, d_zr)
        r[2].wait_recv()
        v = W.at[0, z, yl, HI]
        f2 = send(v, v, d_yr)
        r[1].wait_recv()
        v = W.at[1, zr, y, LO]
        f1 = send(v, v, d_zl)
        r[3].wait_recv()
        v = W.at[1, z, yr, HI]
        f3 = send(v, v, d_yl)
        ag[c, 2] = (f0, f1, f2, f3)

    def ag3(c):
        W, r = Ws[c], ag[c, 2]
        r[0].wait_recv()
        r[1].wait_recv()
        a = W.at[:, :, y, LO]
        f0, f1 = send(a, a, d_yr), send(a, a, d_yl)
        r[2].wait_recv()
        r[3].wait_recv()
        b = W.at[:, z, :, HI]
        ag[c, 3] = (f0, f1, send(b, b, d_zr), send(b, b, d_zl))

    def ag4(c):
        W, r = Ws[c], ag[c, 3]
        r[0].wait_recv()
        v = W.at[0, :, yl, LO]
        f0 = send(v, v, d_yr)
        r[2].wait_recv()
        v = W.at[0, zl, :, HI]
        f2 = send(v, v, d_zr)
        r[1].wait_recv()
        v = W.at[1, :, yr, LO]
        f1 = send(v, v, d_yl)
        r[3].wait_recv()
        v = W.at[1, zr, :, HI]
        f3 = send(v, v, d_zl)
        ag[c, 4] = (f0, f1, f2, f3)

    def ag5(c):
        for copy in ag[c, 4]:
            copy.wait_recv()

    def ag1_direct(c):
        W = Ws[c]
        ag[c, 0].wait_recv()
        a, b = W.at[:, z, y, LO], W.at[:, z, y, HI]
        ag[c, 1] = [send(a, a, d) for d in ring_z], [send(b, b, d) for d in ring_y]

    def ag2_direct(c):
        W = Ws[c]
        for copy in ag[c, 1][0]:
            copy.wait_recv()
        a = W.at[:, :, y, LO]
        first = [send(a, a, d) for d in ring_y]
        for copy in ag[c, 1][1]:
            copy.wait_recv()
        b = W.at[:, z, :, HI]
        ag[c, 4] = first + [send(b, b, d) for d in ring_z]

    rs = {}

    def add(ref, index, *others):
        total = ref[index].astype(F32)
        for other in others:
            total = total + other.astype(F32).reshape(total.shape)
        ref[index] = total.astype(BF)

    lo, hi = slice(0, 16), slice(16, 32)
    every = slice(None)

    def one(i):
        return pl.ds(i, 1)

    def rs1(c):
        G, ra = Gs[c], RA[c]
        rs[c, 1] = (
            send(G.at[0, :, yo, LO], ra.at[0, 0], d_yr),
            send(G.at[1, :, yo, LO], ra.at[0, 1], d_yl),
            send(G.at[0, zo, :, HI], ra.at[1, 0], d_zr),
            send(G.at[1, zo, :, HI], ra.at[1, 1], d_zl),
        )

    def rs2(c):
        G, ra, rb, r = Gs[c], RA[c], RB[c], rs[c, 1]
        r[0].wait_recv()
        add(G, (0, every, one(yr), lo), ra[0, 0])
        f0 = send(G.at[:, :, yr, LO], rb.at[0, 0], d_yr)
        r[2].wait_recv()
        add(G, (0, one(zr), every, hi), ra[1, 0])
        f2 = send(G.at[:, zr, :, HI], rb.at[1, 0], d_zr)
        r[1].wait_recv()
        add(G, (1, every, one(yl), lo), ra[0, 1])
        f1 = send(G.at[:, :, yl, LO], rb.at[0, 1], d_yl)
        r[3].wait_recv()
        add(G, (1, one(zl), every, hi), ra[1, 1])
        f3 = send(G.at[:, zl, :, HI], rb.at[1, 1], d_zl)
        rs[c, 2] = (f0, f1, f2, f3)

    def rs3(c):
        G, rb, rc, r = Gs[c], RB[c], RC[c], rs[c, 2]
        r[0].wait_recv()
        r[1].wait_recv()
        add(G, (every, every, one(y), lo), rb[0, 0], rb[0, 1])
        f0 = send(G.at[0, zo, y, LO], rc.at[0, 0], d_zr)
        f1 = send(G.at[1, zo, y, LO], rc.at[0, 1], d_zl)
        r[2].wait_recv()
        r[3].wait_recv()
        add(G, (every, one(z), every, hi), rb[1, 0], rb[1, 1])
        f2 = send(G.at[0, z, yo, HI], rc.at[1, 0], d_yr)
        f3 = send(G.at[1, z, yo, HI], rc.at[1, 1], d_yl)
        rs[c, 3] = (f0, f1, f2, f3)

    def rs4(c):
        G, rc, rd, r = Gs[c], RC[c], RD[c], rs[c, 3]
        r[0].wait_recv()
        add(G, (0, one(zr), one(y), lo), rc[0, 0])
        f0 = send(G.at[:, zr, y, LO], rd.at[0, 0], d_zr)
        r[2].wait_recv()
        add(G, (0, one(z), one(yr), hi), rc[1, 0])
        f2 = send(G.at[:, z, yr, HI], rd.at[1, 0], d_yr)
        r[1].wait_recv()
        add(G, (1, one(zl), one(y), lo), rc[0, 1])
        f1 = send(G.at[:, zl, y, LO], rd.at[0, 1], d_zl)
        r[3].wait_recv()
        add(G, (1, one(z), one(yl), hi), rc[1, 1])
        f3 = send(G.at[:, z, yl, HI], rd.at[1, 1], d_yl)
        rs[c, 4] = (f0, f1, f2, f3)

    def rs5(c):
        G, rd, r = Gs[c], RD[c], rs[c, 4]
        for copy in r:
            copy.wait_recv()
        add(G, (every, one(z), one(y), lo), rd[0, 0], rd[0, 1])
        add(G, (every, one(z), one(y), hi), rd[1, 0], rd[1, 1])
        rs[c, 5] = send(G.at[xo, z, y], RE[c], d_x)

    def rs6(c):
        rs[c, 5].wait_recv()
        total = Gs[c][x, z, y].astype(F32) + RE[c][...].astype(F32)
        if c == 0:
            gq_w[...] = total[:, 0:256]
            gk_w[...] = total[:, 256:384]
            gv_w[...] = total[:, 384:512]
        elif c == OUT:
            go_w[...] = total
        else:
            w, o = FF_PARTS[c - 1], FF_OFF[c - 1]
            gg_w[:, o : o + w] = total[:, 0:w]
            gu_w[:, o : o + w] = total[:, w : 2 * w]
            gd_w[:, o : o + w] = total[:, 2 * w : 3 * w]

    def rs1_direct(c):
        G, rb = Gs[c], RB[c]
        a = [send(G.at[:, :, i, LO], rb.at[0, k], d) for k, (i, d) in enumerate(zip((yr, yl, yo), ring_y))]
        b = [send(G.at[:, i, :, HI], rb.at[1, k], d) for k, (i, d) in enumerate(zip((zr, zl, zo), ring_z))]
        rs[c, 2] = a, b

    def rs3_direct(c):
        G, rb, rd, (a, b) = Gs[c], RB[c], RD[c], rs[c, 2]
        for copy in a:
            copy.wait_recv()
        add(G, (every, every, one(y), lo), rb[0, 0], rb[0, 1], rb[0, 2])
        a = [send(G.at[:, i, y, LO], rd.at[0, k], d) for k, (i, d) in enumerate(zip((zr, zl, zo), ring_z))]
        for copy in b:
            copy.wait_recv()
        add(G, (every, one(z), every, hi), rb[1, 0], rb[1, 1], rb[1, 2])
        b = [send(G.at[:, z, i, HI], rd.at[1, k], d) for k, (i, d) in enumerate(zip((yr, yl, yo), ring_y))]
        rs[c, 4] = a + b

    def rs5_direct(c):
        G, rd = Gs[c], RD[c]
        for copy in rs[c, 4]:
            copy.wait_recv()
        add(G, (every, one(z), one(y), lo), rd[0, 0], rd[0, 1], rd[0, 2])
        add(G, (every, one(z), one(y), hi), rd[1, 0], rd[1, 1], rd[1, 2])
        rs[c, 5] = send(G.at[xo, z, y], RE[c], d_x)

    def rows_start(buf):
        v = buf.at[t]
        return send(v, v, d_o), send(v, v, d_s)

    def rows_relay(buf, pair):
        pair[0].wait_recv()
        v = buf.at[to]
        return send(v, v, d_s)

    def rows_end(pair, relay):
        pair[1].wait_recv()
        relay.wait_recv()

    def sum_far(k, part):
        PB[k, td] = part(td)
        copy = send(PB.at[k, td], T1.at[k, 1], d_s)
        PB[k, to] = part(to)
        return (copy,)

    def sum_near(k, part):
        PB[k, ts] = part(ts)
        copy = send(PB.at[k, ts], T1.at[k, 0], d_s)
        PB[k, t] = part(t)
        return (copy,)

    def sum_start(k, part):
        return sum_far(k, part) + sum_near(k, part)

    def sum_mid(k, copies):
        copies[0].wait_recv()
        PB[k, to] = (PB[k, to].astype(F32) + T1[k, 1].astype(F32)).astype(BF)
        return send(PB.at[k, to], T2.at[k], d_o)

    def sum_end(k, copies, last):
        copies[1].wait_recv()
        part = PB[k, t].astype(F32) + T1[k, 0].astype(F32)
        last.wait_recv()
        return part + T2[k].astype(F32)

    barrier = pltpu.get_barrier_semaphore()
    for device in partners:
        pl.semaphore_signal(barrier, inc=1, device_id=device, device_id_type=MESH)

    W0 = Ws[0]
    W0[x, z, y, :, 0:256] = wq[...]
    W0[x, z, y, :, 256:384] = wk[...]
    W0[x, z, y, :, 384:512] = wv[...]
    W0[x, z, y, :, 512:768] = wo[...]
    for c in range(1, CHUNKS):
        w, o = FF_PARTS[c - 1], FF_OFF[c - 1]
        Ws[c][x, z, y, :, 0:w] = wg[:, o : o + w]
        Ws[c][x, z, y, :, w : 2 * w] = wu[:, o : o + w]
        Ws[c][x, z, y, :, 2 * w : 3 * w] = wd[:, o : o + w]
    n1, _ = rms(tok[...].astype(F32))
    A1[t] = (n1 * na[...]).astype(BF)
    GO[t] = cot[...]

    pl.semaphore_wait(barrier, len(partners))

    ag0(0)
    a1_pair = rows_start(A1)
    for c in range(1, CHUNKS):
        ag0(c)

    lane = lax.broadcasted_iota(jnp.int32, (1, 128), 1)
    left_head = lane < 64
    first_half = (lane % 64) < 32

    e1 = lens[0, 0]
    e2 = e1 + lens[0, 1]
    e3 = e2 + lens[0, 2]

    def begin(row):
        return jnp.where(
            row >= e3, e3, jnp.where(row >= e2, e2, jnp.where(row >= e1, e1, 0))
        )

    def fill_tables(i, carry):
        rows = pl.ds(pl.multiple_of(i * 128, 128), 128)
        row = lax.broadcasted_iota(jnp.int32, (128, 128), 0) + i * 128
        angle = (row - begin(row)).astype(F32) * fr[...]
        COS[rows] = jnp.cos(angle)
        SIN[rows] = jnp.where(first_half, -1.0, 1.0) * jnp.sin(angle)
        return carry

    def fill_bias(i, carry):
        rows = pl.ds(pl.multiple_of(i * 128, 128), 128)
        row = lax.broadcasted_iota(jnp.int32, (128, 512), 0) + i * 128
        col = lax.broadcasted_iota(jnp.int32, (128, 512), 1)
        seen = (col <= row) & (col >= begin(row))
        BIAS[rows] = jnp.where(seen, 0.0, -1e30)
        return carry

    lax.fori_loop(0, 2, fill_tables, 0)
    ag1_direct(0)
    lax.fori_loop(2, 4, fill_tables, 0)
    ag2_direct(0)
    a1_relay = rows_relay(A1, a1_pair)
    for c in range(1, CHUNKS):
        ag1(c)
    lax.fori_loop(0, 4, fill_bias, 0)
    rows_end(a1_pair, a1_relay)
    A1T[...] = A1[...].reshape(512, D).T
    for c in range(1, CHUNKS):
        ag2(c)
    ag3(1)
    ag5(0)
    go_pair = rows_start(GO)
    for c in range(2, CHUNKS):
        ag3(c)

    def rope(v, rows):
        swapped = jnp.where(first_half, pltpu.roll(v, 96, 1), pltpu.roll(v, 32, 1))
        return v * COS[rows] + swapped * SIN[rows]

    def rope_back(v, rows):
        swapped = jnp.where(first_half, pltpu.roll(v, 96, 1), pltpu.roll(v, 32, 1))
        return v * COS[rows] - swapped * SIN[rows]

    hr = lax.broadcasted_iota(jnp.int32, (128, 128), 0) // 64
    hc = lax.broadcasted_iota(jnp.int32, (128, 128), 1) // 64
    mean_of = jnp.where(hr == hc, 1.0 / HD, 0.0).astype(BF)

    def head_mean(v):
        high = v.astype(BF)
        low = (v - high.astype(F32)).astype(BF)
        return dot(high, mean_of) + dot(low, mean_of)

    q_gain = jnp.concatenate([qg[...], qg[...]], axis=1)
    k_gain = jnp.concatenate([kg[...], kg[...]], axis=1)

    def qkv_block(i, carry):
        rows = pl.ds(pl.multiple_of(i * 256, 256), 256)
        raw = dot(A1[pl.ds(2 * i, 2)].reshape(256, D), W0[:, :, :, :, 0:512].reshape(D, 512))
        for g in range(3):
            v = raw[:, 128 * g : 128 * g + 128]
            inverse = lax.rsqrt(head_mean(v * v) + EPS)
            n = v * inverse
            NQ[g, rows] = n
            RQ[g, rows] = inverse
            r = rope(n * (q_gain if g < 2 else k_gain), rows)
            if g < 2:
                QS[g, rows] = (r * HD**-0.5).astype(BF)
            else:
                turned = pltpu.roll(r, 64, 1)
                KD[0, rows] = jnp.where(left_head, r, turned).astype(BF)
                KD[1, rows] = jnp.where(left_head, turned, r).astype(BF)
        v = raw[:, 384:512]
        turned = pltpu.roll(v, 64, 1)
        VD[0, rows] = jnp.where(left_head, v, turned).astype(BF)
        VD[1, rows] = jnp.where(left_head, turned, v).astype(BF)
        return carry

    lax.fori_loop(0, 2, qkv_block, 0)

    def stack(v):
        none = jnp.zeros_like(v)
        return jnp.concatenate(
            [jnp.where(left_head, v, none), jnp.where(left_head, none, v)], axis=0
        )

    def unstack(v):
        half = v.shape[0] // 2
        return jnp.where(left_head, v[:half], v[half:])

    def attend(g, i):
        rows = pl.ds(pl.multiple_of(i * 256, 256), 256)
        scores = dot_nt(stack(QS[g, rows]), KD[g])
        bias = BIAS[rows]
        scores = scores + jnp.concatenate([bias, bias], axis=0)
        expo = jnp.exp(scores - jnp.max(scores, axis=-1, keepdims=True))
        probs = expo * (1.0 / jnp.sum(expo, axis=-1, keepdims=True))
        PR[g, pl.ds(pl.multiple_of(i * 512, 512), 512)] = probs
        O[rows, 128 * g : 128 * g + 128] = unstack(dot(probs.astype(BF), VD[g])).astype(BF)

    here = t // 2
    there = 1 - here

    def out_part(b):
        rows = pl.ds(pl.multiple_of(b * 128, 128), 128)
        return dot_nt(O[rows], W0[:, :, :, :, 512:768].reshape(D, 256)).astype(BF)

    attend(0, there)
    attend(1, there)
    at_copies = sum_far(0, out_part)
    ag4(1)
    go_relay = rows_relay(GO, go_pair)
    attend(0, here)
    at_last = sum_mid(0, at_copies)
    attend(1, here)
    at_copies += sum_near(0, out_part)
    rows_end(go_pair, go_relay)
    GOT[...] = GO[...].reshape(512, D).T
    ag4(2)
    x2 = tok[...].astype(F32) + sum_end(0, at_copies, at_last)
    X2[...] = x2
    n2, _ = rms(x2)
    A2[t] = (n2 * nf[...]).astype(BF)
    a2_pair = rows_start(A2)
    ag5(1)
    for c in range(3, CHUNKS):
        ag4(c)

    def ffn_chunk(c, i):
        W = Ws[c]
        w, o = FF_PARTS[c - 1], FF_OFF[c - 1]
        cols = slice(o, o + w)

        rows = pl.ds(pl.multiple_of(i * 256, 256), 256)
        a = A2[pl.ds(2 * i, 2)].reshape(256, D)
        g = GO[pl.ds(2 * i, 2)].reshape(256, D)
        gate = dot(a, W[:, :, :, :, 0:w].reshape(D, w))
        up = dot(a, W[:, :, :, :, w : 2 * w].reshape(D, w))
        dhid = dot(g, W[:, :, :, :, 2 * w : 3 * w].reshape(D, w))
        sigma = jax.nn.sigmoid(gate)
        swish = gate * sigma
        HID[rows, cols] = (swish * up).astype(BF)
        dgate = (dhid * up * sigma * (1.0 + gate * (1.0 - sigma))).astype(BF)
        dup = (dhid * swish).astype(BF)
        DG[rows, cols] = dgate
        DU[rows, cols] = dup
        part = dot_nt(dgate, W[:, :, :, :, 0:w].reshape(D, w)) + dot_nt(
            dup, W[:, :, :, :, w : 2 * w].reshape(D, w)
        )
        if c == 1:
            DA[rows] = part
        else:
            DA[rows] = DA[rows] + part

    def ffn_grads(c):
        G = Gs[c]
        w, o = FF_PARTS[c - 1], FF_OFF[c - 1]
        cols = slice(o, o + w)

        def block(i, carry):
            rows = pl.ds(pl.multiple_of(i * 256, 256), 256)
            zs = pl.ds(2 * (i % 2), 2)
            a, g = A2T[rows], GOT[rows]
            G[i // 2, zs, :, :, 0:w] = dot(a, DG[:, cols]).astype(BF).reshape(2, 4, 32, w)
            G[i // 2, zs, :, :, w : 2 * w] = dot(a, DU[:, cols]).astype(BF).reshape(2, 4, 32, w)
            G[i // 2, zs, :, :, 2 * w : 3 * w] = dot(g, HID[:, cols]).astype(BF).reshape(2, 4, 32, w)
            return carry

        lax.fori_loop(0, 4, block, 0)

    def da2_part(b):
        rows = pl.ds(pl.multiple_of(b * 128, 128), 128)
        return DA[rows].astype(BF)

    a2_pair[1].wait_recv()
    ffn_chunk(1, here)
    a2_relay = rows_relay(A2, a2_pair)
    ag5(2)
    ffn_chunk(2, here)
    a2_relay.wait_recv()
    A2T[...] = A2[...].reshape(512, D).T
    ffn_chunk(1, there)
    ffn_grads(1)
    rs1(1)
    for c in range(2, CHUNKS):
        if c > 2:
            ag5(c)
        ffn_chunk(c, there)
        if c + 1 == CHUNKS:
            da2_copies = sum_far(1, da2_part)
        if c > 2:
            ffn_chunk(c, here)
    da2_copies += sum_near(1, da2_part)
    da2_last = sum_mid(1, da2_copies)
    rs2(1)
    for c in range(2, CHUNKS):
        ffn_grads(c)
        rs1(c)

    def y_part(b):
        rows = pl.ds(pl.multiple_of(b * 128, 128), 128)
        total = None
        for c in range(1, CHUNKS):
            w, o = FF_PARTS[c - 1], FF_OFF[c - 1]
            part = dot_nt(HID[rows, o : o + w], Ws[c][:, :, :, :, 2 * w : 3 * w].reshape(D, w))
            total = part if total is None else total + part
        return total.astype(BF)

    rs2(2)
    da2 = sum_end(1, da2_copies, da2_last)
    n2, r2 = rms(X2[...])
    GVA[pl.ds(slot, 1), :, 1024:2048] = jnp.sum(da2 * n2, axis=0, keepdims=True).reshape(1, 1, D)
    h = da2 * nf[...]
    dx2 = cot[...].astype(F32) + r2 * (h - n2 * jnp.mean(h * n2, axis=-1, keepdims=True))
    DX2[...] = dx2
    GX[t] = dx2.astype(BF)
    gx_pair = rows_start(GX)
    y_copies = sum_far(2, y_part)

    def do_block(i):
        rows = pl.ds(pl.multiple_of(i * 256, 256), 256)
        g = GX[pl.ds(2 * i, 2)].reshape(256, D)
        DO[rows] = dot(g, W0[:, :, :, :, 512:768].reshape(D, 256)).astype(BF)

    def attend_back(g, i, first):
        rows = pl.ds(pl.multiple_of(i * 256, 256), 256)
        qs = stack(QS[g, rows])
        dos = stack(DO[rows, 128 * g : 128 * g + 128])
        probs = PR[g, pl.ds(pl.multiple_of(i * 512, 512), 512)]
        dprob = dot_nt(dos, VD[g])
        ds = probs * (dprob - jnp.sum(probs * dprob, axis=-1, keepdims=True))
        low = ds.astype(BF)
        DQ[g, rows] = unstack(dot(low, KD[g])) * HD**-0.5
        dk = dot_tn(low, qs)
        dv = dot_tn(probs.astype(BF), dos)
        if first:
            DK[g] = dk
            DV[g] = dv
        else:
            DK[g] = DK[g] + dk
            DV[g] = DV[g] + dv

    gx_pair[1].wait_recv()
    do_block(here)
    attend_back(0, here, True)
    gx_relay = rows_relay(GX, gx_pair)
    attend_back(1, here, True)
    y_copies += sum_near(2, y_part)
    for c in range(3, CHUNKS):
        rs2(c)
    gx_relay.wait_recv()
    do_block(there)
    Gs[OUT][...] = dot_tn(GX[...].reshape(512, D), O[...]).astype(BF).reshape(2, 4, 4, 32, 256)
    rs1_direct(OUT)
    attend_back(0, there, False)
    rs3(1)
    attend_back(1, there, False)
    rs3(2)

    def raw_grads(i, carry):
        rows = pl.ds(pl.multiple_of(i * 256, 256), 256)
        dks = DK[:, rows]
        dvs = DV[:, rows]
        dk = jnp.where(left_head, dks[0] + pltpu.roll(dks[0], 64, 1), dks[1] + pltpu.roll(dks[1], 64, 1))
        dv = jnp.where(left_head, dvs[0] + pltpu.roll(dvs[0], 64, 1), dvs[1] + pltpu.roll(dvs[1], 64, 1))
        DQKV[rows, 384:512] = dv.astype(BF)
        sums = []
        for g in range(3):
            e = rope_back(DQ[g, rows] if g < 2 else dk, rows)
            n = NQ[g, rows]
            sums.append(jnp.sum(e * n, axis=0, keepdims=True))
            eg = e * (q_gain if g < 2 else k_gain)
            DQKV[rows, 128 * g : 128 * g + 128] = (
                RQ[g, rows] * (eg - n * head_mean(eg * n))
            ).astype(BF)
        return carry[0] + sums[0] + sums[1], carry[1] + sums[2]

    zero = jnp.zeros((1, 128), F32)
    sum_q, sum_k = lax.fori_loop(0, 2, raw_grads, (zero, zero))
    GVA[pl.ds(slot, 1), :, 2048:2176] = sum_q.reshape(1, 1, 128)
    GVA[pl.ds(slot, 1), :, 2176:2304] = sum_k.reshape(1, 1, 128)

    G0 = Gs[0]

    def attn_grads(i, carry):
        rows = pl.ds(pl.multiple_of(i * 256, 256), 256)
        zs = pl.ds(2 * (i % 2), 2)
        G0[i // 2, zs, :, :, 0:512] = dot(A1T[rows], DQKV[...]).astype(BF).reshape(2, 4, 32, 512)
        return carry

    def da1_part(b):
        rows = pl.ds(pl.multiple_of(b * 128, 128), 128)
        return dot_nt(DQKV[rows], W0[:, :, :, :, 0:512].reshape(D, 512)).astype(BF)

    da1_copies = sum_start(3, da1_part)
    lax.fori_loop(0, 4, attn_grads, 0)
    rs1_direct(0)
    da1_last = sum_mid(3, da1_copies)
    rs3_direct(OUT)
    rs4(1)
    for c in range(3, CHUNKS):
        rs3(c)
    y_last = sum_mid(2, y_copies)
    rs4(2)
    rs5(1)
    rs3_direct(0)
    rs5_direct(OUT)
    for c in range(3, CHUNKS):
        rs4(c)
    rs5(2)
    da1 = sum_end(3, da1_copies, da1_last)
    n1, r1 = rms(tok[...].astype(F32))
    GVA[pl.ds(slot, 1), :, 0:1024] = jnp.sum(da1 * n1, axis=0, keepdims=True).reshape(1, 1, D)
    mine = GVA.at[slot]
    g_copies = [send(mine, mine, device) for device in near]
    h = da1 * na[...]
    gtok[...] = DX2[...] + r1 * (h - n1 * jnp.mean(h * n1, axis=-1, keepdims=True))
    rs5_direct(0)

    def total_of(ref, count, copies):
        for copy in copies:
            copy.wait_recv()
        total = ref[0]
        for i in range(1, count):
            total = total + ref[i]
        return total

    GVB[pl.ds(z * 4 + y, 1)] = total_of(GVA, 8, g_copies).reshape(1, 1, GAINS)
    mine = GVB.at[z * 4 + y]
    g_copies = [send(mine, mine, device) for device in plane]
    for c in range(3, CHUNKS):
        rs5(c)
    out[...] = (X2[...] + sum_end(2, y_copies, y_last)).astype(BF)
    for c in range(1, CHUNKS):
        rs6(c)
    rs6(OUT)
    rs6(0)
    total = total_of(GVB, 16, g_copies)
    turned = pltpu.roll(total[:, 2048:2304], 192, 1) + total[:, 2048:2304]
    gna[...] = total[:, 0:1024]
    gnf[...] = total[:, 1024:2048]
    gqg[...] = turned[:, 0:64]
    gkg[...] = turned[:, 128:192]

    for copy in started:
        copy.wait_send()


def hand_on(*refs):
    count = len(refs) // 2
    sems = refs[-1]
    copies = [
        pltpu.make_async_copy(refs[i], refs[count + i], sems.at[i]) for i in range(count)
    ]
    for copy in copies:
        copy.start()
    for copy in copies:
        copy.wait()


def on_device(
    tokens, seq_lens, norm_attn, w_query, w_key, w_value, w_out, query_gain, key_gain,
    norm_ffn, w_gate, w_up, w_down, cotangent,
):
    freq = np.exp(-math.log(THETA) * 2.0 * np.arange(HD // 2, dtype=np.float64) / HD)
    freq = jnp.asarray(np.tile(freq.astype(np.float32), 4)[None, :])
    shape = jax.ShapeDtypeStruct
    vmem = pl.BlockSpec(memory_space=pltpu.VMEM)
    outs = (
        shape((128, D), BF),
        shape((128, D), F32),
        shape((32, 256), F32),
        shape((32, 128), F32),
        shape((32, 128), F32),
        shape((32, 256), F32),
        shape((32, FFL), F32),
        shape((32, FFL), F32),
        shape((32, FFL), F32),
        shape((1, D), F32),
        shape((1, D), F32),
        shape((1, HD), F32),
        shape((1, HD), F32),
    )
    V = pltpu.VMEM
    scratch = [
        [V((2, 4, 4, 32, w), BF) for w in WIDTHS],
        [V((2, 4, 4, 32, w), BF) for w in SUMS],
        [V((2, 2, 4, 16, w) if 0 < i < OUT else (16, 128), BF) for i, w in enumerate(SUMS)],
        [V((2, 2 if 0 < i < OUT else 3, 2, 4, 16, w), BF) for i, w in enumerate(SUMS)],
        [V((2, 2, 16, w) if 0 < i < OUT else (16, 128), BF) for i, w in enumerate(SUMS)],
        [V((2, 2 if 0 < i < OUT else 3, 2, 16, w), BF) for i, w in enumerate(SUMS)],
        [V((32, w), BF) for w in SUMS],
        V((4, 128, D), BF),
        V((4, 128, D), BF),
        V((4, 128, D), BF),
        V((4, 128, D), BF),
        V((D, 512), BF),
        V((D, 512), BF),
        V((D, 512), BF),
        V((4, 4, 128, D), BF),
        V((4, 2, 128, D), BF),
        V((4, 128, D), BF),
        V((128, D), F32),
        V((128, D), F32),
        V((512, 128), F32),
        V((512, 128), F32),
        V((512, 512), F32),
        V((3, 512, 128), F32),
        V((3, 512, 128), F32),
        V((2, 512, 128), BF),
        V((2, 512, 128), BF),
        V((2, 512, 128), BF),
        V((2, 1024, 512), F32),
        V((512, 256), BF),
        V((512, 256), BF),
        V((2, 512, 128), F32),
        V((2, 512, 128), F32),
        V((2, 512, 128), F32),
        V((512, 512), BF),
        V((512, FFL), BF),
        V((512, FFL), BF),
        V((512, FFL), BF),
        V((512, D), F32),
        V((8, 1, GAINS), F32),
        V((16, 1, GAINS), F32),
        pltpu.SemaphoreType.DMA((NSEM,)),
        pltpu.SemaphoreType.DMA((NSEM,)),
    ]
    r = pl.pallas_call(
        kernel,
        out_shape=outs,
        in_specs=[pl.BlockSpec(memory_space=pltpu.SMEM)] + [vmem] * 14,
        out_specs=[vmem] * len(outs),
        scratch_shapes=scratch,
        compiler_params=pltpu.CompilerParams(
            collective_id=0, has_side_effects=True, vmem_limit_bytes=63 * 2**20
        ),
        name="layer",
    )(
        seq_lens, tokens, cotangent, w_query, w_key, w_value, w_out.T, w_gate, w_up, w_down.T,
        norm_attn[None], norm_ffn[None], query_gain[None], key_gain[None], freq,
    )
    anywhere = pl.BlockSpec(memory_space=pl.ANY)
    r = pl.pallas_call(
        hand_on,
        out_shape=outs,
        in_specs=[vmem] * len(outs),
        out_specs=[anywhere] * len(outs),
        scratch_shapes=[pltpu.SemaphoreType.DMA((len(outs),))],
        name="hand_on",
    )(*r)
    out, gtok, gq, gk, gv, go, gg, gu, gd, gna, gnf, gqg, gkg = r
    return (out, gtok, gna[0], gq, gk, gv, go.T, gqg[0], gkg[0], gnf[0], gg, gu, gd.T)


def solution(mesh):
    rows = P(("dp", "tensor"), None)
    split, across, full = P("dp", "tensor"), P("tensor", "dp"), P()
    return jax.shard_map(
        on_device,
        mesh=mesh,
        in_specs=(
            rows, P("dp", None), full, split, split, split, across, full, full, full,
            split, split, across, rows,
        ),
        out_specs=(
            rows, rows, full, split, split, split, across, full, full, full, split, split, across,
        ),
        check_vma=False,
    )
```
